256 devices in a mesh: seq: 64 (over y, z, core), head: 4 (over x).
Axes of the slice: x: 4, y: 4, z: 8, core: 2. Of those that a mesh axis runs over, the one named last changes fastest.
Arguments:
- queries: bfloat16 [196608, 1024], P('seq', 'head'), may hold values from -5 to 5
- keys: bfloat16 [196608, 128], P('seq'), may hold values from -5 to 5
- values: bfloat16 [196608, 128], P('seq'), may hold values from -6 to 6
- selected: int32 [384, 3], P('seq'), may hold values from 0 to 382, as said below
Outputs:
- attended: bfloat16 [196608, 1024], P('seq', 'head')
The draws below stay inside these ranges and needn't reach their ends.
Inputs may be any that keep to these rules, and one draw needn't show every extreme that they name: Every nonzero selected[b, j] is a block before b. The selections of the 6 query blocks held by one index of seq name at most one block of each other index. A 0 marks an empty slot.
All inputs are finite; a program needn't handle non-finite values.
Results may differ from the reference program's by a relative error of at most 0.0049.
Values may be sent and summed in bfloat16 or wider, within the bound.
A program may use at most 128 MiB of HBM per device.

```python
import math
import jax
import jax.numpy as jnp
from jax import lax

DH = 128
HQ = 8
BLK = 512
TOPK = 3
QB_DEV = 6
N_BLOCKS = 384
TOKENS = 196608


def draw_queries(key, part):
    key = jax.random.fold_in(key, 11)
    base = jnp.clip(jax.random.normal(key, (TOKENS, HQ * DH), jnp.float32), -5.0, 5.0)
    return base.astype(jnp.bfloat16)


def draw_keys(key, part):
    key = jax.random.fold_in(key, 12)
    base = jnp.clip(jax.random.normal(key, (TOKENS, DH), jnp.float32), -5.0, 5.0)
    return base.astype(jnp.bfloat16)


def draw_selected(key, part):
    key = jax.random.fold_in(key, 13)
    first, second, third, fourth = jax.random.split(key, 4)
    devices = N_BLOCKS // QB_DEV
    count = QB_DEV * TOPK
    device = jnp.arange(devices, dtype=jnp.int32)[:, None]
    last_device = device == devices - 1
    span = jnp.maximum(device, 1)
    rotate = jax.random.randint(first, (devices, 1), 0, 1 << 20) % span
    rotate = jnp.where(last_device, 0, rotate)
    ranking = jax.random.randint(second, (devices, count), 0, 1 << 16) * count + jnp.arange(count, dtype=jnp.int32)[None, :]
    ticket = jnp.argsort(ranking, axis=1).astype(jnp.int32)
    query = jnp.arange(count, dtype=jnp.int32)[None, :] // TOPK
    remote_owner = (rotate + ticket) % span
    remote_block = remote_owner * QB_DEV + jax.random.randint(third, (devices, count), 0, QB_DEV)
    remote_block = jnp.where(last_device & (ticket == 0), 1, remote_block)
    picked = jax.random.randint(fourth, (devices, count), 0, 1 << 20) % jnp.maximum(query, 1)
    local_block = jnp.where(query > 0, device * QB_DEV + picked, 0)
    result = jnp.where(ticket < device, remote_block, local_block)
    result = result.reshape(N_BLOCKS, TOPK).astype(jnp.int32)
    previous = result[N_BLOCKS - 1, 0]
    result = result.at[N_BLOCKS - 1, 0].set(N_BLOCKS - 2)
    moved = jnp.where(previous == 1, 1, result[N_BLOCKS - 1, 1]).astype(jnp.int32)
    return result.at[N_BLOCKS - 1, 1].set(moved)


def shard_levels(rng, extent, pieces, smallest, top_value):
    level = 1.0
    for axis_at, blocks in pieces:
        heights = jax.random.uniform(jax.random.fold_in(jax.random.fold_in(rng, 6), axis_at), (blocks,), jnp.float32, smallest / len(pieces), top_value / len(pieces))
        level = level * jnp.repeat(jnp.exp(heights), extent[axis_at] // blocks).reshape((-1,) + (1,) * (len(extent) - 1 - axis_at))
    return level


def centred(key, shape, width, most, cuts=(), kind=jnp.bfloat16):
    array = width * jax.random.normal(key, shape, jnp.float32)
    if cuts:
        array = array * shard_levels(key, shape, cuts, -0.22, 0.18)
    return jnp.clip(array, -most, most).astype(kind)


def setup_inputs(seed: int = 0) -> dict:
    seeds = jax.random.split(jax.random.key(seed), 5)
    return {
        "queries": draw_queries(jax.random.fold_in(seeds[4], 71), 0),
        "keys": draw_keys(jax.random.fold_in(seeds[4], 71), 0),
        "values": centred(seeds[2], (TOKENS, DH), 1.0, 6.0, ((0, 64),)),
        "selected": draw_selected(jax.random.fold_in(seeds[4], 71), 0),
    }


def live_slots(chosen):
    nonzero = chosen != 0
    equal = chosen[:, :, None] == chosen[:, None, :]
    order = jnp.arange(chosen.shape[1])
    earlier = order[None, :] < order[:, None]
    repeated = jnp.any(equal & earlier[None, :, :], axis=2)
    return nonzero & jnp.logical_not(repeated)

def reference(queries, keys, values, selected):
    query_blocks = queries.reshape(N_BLOCKS, BLK, HQ, DH)
    key_blocks = keys.reshape(N_BLOCKS, BLK, DH)
    value_blocks = values.reshape(N_BLOCKS, BLK, DH)
    live = live_slots(selected)
    scale = 1.0 / math.sqrt(DH)
    position = jnp.arange(BLK)
    causal = position[None, :] <= position[:, None]

    def one_block(number):
        chosen = selected[number]
        tiles_k = jnp.concatenate([key_blocks[0][None], key_blocks[number][None], key_blocks[chosen]], axis=0)
        tiles_v = jnp.concatenate([value_blocks[0][None], value_blocks[number][None], value_blocks[chosen]], axis=0)
        tiles_k = tiles_k.reshape((TOPK + 2) * BLK, DH).astype(jnp.float32)
        tiles_v = tiles_v.reshape((TOPK + 2) * BLK, DH).astype(jnp.float32)
        tile_live = jnp.concatenate([jnp.reshape(number != 0, (1,)), jnp.ones((1,), bool), live[number]])
        allowed = jnp.broadcast_to(tile_live[None, :, None], (BLK, TOPK + 2, BLK))
        allowed = allowed.at[:, 1, :].set(causal)
        allowed = allowed.reshape(BLK, (TOPK + 2) * BLK)
        query_here = query_blocks[number].astype(jnp.float32)
        scores = jnp.einsum('qhd,kd->hqk', query_here, tiles_k) * scale
        scores = jnp.where(allowed[None], scores, -1e+30)
        top = lax.optimization_barrier(jnp.max(scores, axis=2, keepdims=True))
        expo = jnp.exp(scores - top)
        total = lax.optimization_barrier(jnp.sum(expo, axis=2, keepdims=True))
        weights = (expo / total).astype(jnp.bfloat16)
        result = jnp.einsum('hqk,kd->qhd', weights.astype(jnp.float32), tiles_v)
        return result.astype(jnp.bfloat16).reshape(BLK, HQ * DH)
    outputs = lax.map(one_block, jnp.arange(N_BLOCKS, dtype=jnp.int32))
    return outputs.reshape(TOKENS, HQ * DH)
```

```python
import functools
import math

import jax
import jax.numpy as jnp
from jax import lax
from jax.experimental import pallas as pl
from jax.experimental.pallas import tpu as pltpu
from jax.sharding import PartitionSpec as P


def live_slots(chosen):
    nonzero = chosen != 0
    equal = chosen[:, :, None] == chosen[:, None, :]
    order = jnp.arange(chosen.shape[1])
    earlier = order[None, :] < order[:, None]
    repeated = jnp.any(equal & earlier[None, :, :], axis=2)
    return nonzero & jnp.logical_not(repeated)


def attend(blocks, parts, slots, tile_ref, q_ref, k_ref, v_ref, got_ref, out_ref, kt, vt, sc):
    block_len, width = q_ref.shape
    head = k_ref.shape[-1]
    rows = block_len // parts
    null = blocks + slots
    step = pl.program_id(0)

    @pl.when(step == 0)
    def _():
        for b in range(blocks):
            kt[b] = k_ref[b]
            vt[b, :, :head] = v_ref[b]
            vt[b, :, head:] = jnp.ones((block_len, head), jnp.bfloat16)
        for s in range(slots):
            for p in range(parts):
                kt[blocks + s, pl.ds(p * rows, rows)] = got_ref[p, s, 0]
                vt[blocks + s, pl.ds(p * rows, rows), :head] = got_ref[p, s, 1]
            vt[blocks + s, :, head:] = jnp.ones((block_len, head), jnp.bfloat16)
        kt[null] = jnp.broadcast_to(got_ref[0, 0, 0, :1, :], (block_len, head))
        vt[null] = jnp.zeros((block_len, 2 * head), jnp.bfloat16)

    factor = math.log2(math.e) / math.sqrt(head)
    half = block_len // 2
    tiles = [tile_ref[step, j] for j in range(4)]
    for h in range(width // head):
        for r in range(2):
            q = q_ref[pl.ds(r * half, half), pl.ds(h * head, head)]
            own = (r + 1) * half

            def score(keys):
                return lax.dot_general(q, keys, (((1,), (1,)), ((), ())), preferred_element_type=jnp.float32)

            s = score(kt[step, :own])
            row = lax.broadcasted_iota(jnp.int32, (half, own), 0) + r * half
            col = lax.broadcasted_iota(jnp.int32, (half, own), 1)
            s = jnp.where(col <= row, s, -1e30)
            sc[:, :own] = s
            top = jnp.max(s, axis=1, keepdims=True)
            for j in range(4):
                s = score(kt[tiles[j]])
                sc[:, pl.ds((j + 1) * block_len, block_len)] = s
                top = jnp.maximum(top, jnp.max(s, axis=1, keepdims=True))
            shift = top * factor
            p = jnp.exp2(sc[:, :own] * factor - shift).astype(jnp.bfloat16)
            acc = jnp.dot(p, vt[step, :own], preferred_element_type=jnp.float32)
            for j in range(4):
                s = sc[:, pl.ds((j + 1) * block_len, block_len)]
                p = jnp.exp2(s * factor - shift).astype(jnp.bfloat16)
                acc += jnp.dot(p, vt[tiles[j]], preferred_element_type=jnp.float32)
            out = acc[:, :head] / acc[:, head:]
            out_ref[pl.ds(r * half, half), pl.ds(h * head, head)] = out.astype(jnp.bfloat16)


def shards(queries, keys, values, selected):
    seq_count = lax.axis_size("seq")
    parts = lax.axis_size("head")
    me = lax.axis_index("seq")
    blocks, per_block = selected.shape
    head = keys.shape[1]
    block_len = keys.shape[0] // blocks
    rows = block_len // parts
    k3 = keys.reshape(blocks, block_len, head)
    v3 = values.reshape(blocks, block_len, head)
    start = lax.axis_index("head") * rows
    mine = jnp.stack(
        [lax.dynamic_slice_in_dim(k3, start, rows, 1), lax.dynamic_slice_in_dim(v3, start, rows, 1)], axis=1
    )
    owner = (selected // blocks).reshape(-1)
    local = (selected % blocks).reshape(-1)
    remote = owner != me
    owner_list = jnp.arange(seq_count, dtype=jnp.int32)
    hits = (owner[:, None] == owner_list[None, :]) & remote[:, None]
    wanted = jnp.sum(jnp.where(hits, local[:, None], 0), axis=0)
    asked = lax.all_to_all(wanted.reshape(seq_count, 1), "seq", 0, 0, tiled=True).reshape(seq_count)
    zero = lax.psum(jnp.where(me == 0, mine[0], 0).astype(jnp.bfloat16), "seq")
    got = lax.all_to_all(mine[asked], "seq", 0, 0, tiled=True)
    packed = jnp.concatenate([zero[None], got[owner]], axis=0)
    slots = packed.shape[0]
    gathered = lax.all_gather(packed, "head")

    live = live_slots(selected)
    numbers = me * blocks + jnp.arange(blocks, dtype=jnp.int32)
    null = blocks + slots
    place = jnp.where(remote, blocks + 1 + jnp.arange(blocks * per_block, dtype=jnp.int32), local)
    place = jnp.where(live, place.reshape(blocks, per_block), null)
    first = jnp.where(numbers != 0, blocks, null)
    tiles = jnp.concatenate([first[:, None], place], axis=1).astype(jnp.int32)

    whole = lambda *shape: pl.BlockSpec(shape, lambda i, t: (0,) * len(shape))
    return pl.pallas_call(
        functools.partial(attend, blocks, parts, slots),
        out_shape=jax.ShapeDtypeStruct(queries.shape, jnp.bfloat16),
        grid_spec=pltpu.PrefetchScalarGridSpec(
            num_scalar_prefetch=1,
            grid=(blocks,),
            in_specs=[
                pl.BlockSpec((block_len, queries.shape[1]), lambda i, t: (i, 0)),
                whole(*k3.shape),
                whole(*v3.shape),
                whole(*gathered.shape),
            ],
            out_specs=pl.BlockSpec((block_len, queries.shape[1]), lambda i, t: (i, 0)),
            scratch_shapes=[
                pltpu.VMEM((null + 1, block_len, head), jnp.bfloat16),
                pltpu.VMEM((null + 1, block_len, 2 * head), jnp.bfloat16),
                pltpu.VMEM((block_len // 2, 5 * block_len), jnp.float32),
            ],
        ),
        compiler_params=pltpu.CompilerParams(vmem_limit_bytes=48 * 2**20),
    )(tiles, queries, k3, v3, gathered)


def solution(mesh):
    in_specs = (P("seq", "head"), P("seq", None), P("seq", None), P("seq", None))
    return jax.shard_map(shards, mesh=mesh, in_specs=in_specs, out_specs=P("seq", "head"), check_vma=False)
```

```python
import functools
import math

import jax
import jax.numpy as jnp
from jax import lax
from jax.experimental import pallas as pl
from jax.experimental.pallas import tpu as pltpu
from jax.sharding import PartitionSpec as P

MESH = pl.DeviceIdType.MESH
NY, NZ, NC, NX = 4, 8, 2, 4
GROUPS = 8
SPAN = 9
ARRIVAL = ((0,), (7, 1), (6, 2), (5, 3), (4,))
PLACE = (0, 2, 4, 6, 7, 5, 3, 1)


def live_slots(chosen):
    nonzero = chosen != 0
    equal = chosen[:, :, None] == chosen[:, None, :]
    order = jnp.arange(chosen.shape[1])
    earlier = order[None, :] < order[:, None]
    repeated = jnp.any(equal & earlier[None, :, :], axis=2)
    return nonzero & jnp.logical_not(repeated)


def exchange(blocks, rows, slots, source_ref, want_smem, want_ref, k_hbm, v_hbm, gk_hbm, gv_hbm, *scratch):
    zs = (scratch[0:8], scratch[8:16])
    sp = scratch[16:18]
    rp = scratch[18:20]
    zero = scratch[20:22]
    xs = scratch[22:24]
    (tabs, tabs_smem, local_sem, tab_local, zsend, zrecv, ysend, yrecv, nsend, nrecv,
     tsend, trecv, xsend, xrecv, xlocal) = scratch[24:]
    hbm = (k_hbm, v_hbm)
    outs = (gk_hbm, gv_hbm)
    s = lax.axis_index("seq")
    x = lax.axis_index("head")
    c = lax.rem(s, NC)
    z = lax.rem(s // NC, NZ)
    y = s // (NC * NZ)

    def at(y2, z2, c2):
        return ((y2 * NZ + z2) * NC + c2, x)

    zr, zl = lax.rem(z + 1, NZ), lax.rem(z + NZ - 1, NZ)
    xr, xl = lax.rem(x + 1, NX), lax.rem(x + NX - 1, NX)
    right, left = at(y, zr, c), at(y, zl, c)
    other = at(y, z, 1 - c)
    x_right, x_left = (s, xr), (s, xl)
    mine = pl.ds(pl.multiple_of(x * rows, rows), rows)

    def remote(src, dst, ss, rs, dev):
        return pltpu.make_async_remote_copy(
            src_ref=src, dst_ref=dst, send_sem=ss, recv_sem=rs, device_id=dev, device_id_type=MESH
        )

    loads = [pltpu.make_async_copy(hbm[p].at[:, mine, :], zs[p][0], local_sem.at[p]) for p in range(2)]
    for copy in loads:
        copy.start()

    barrier = pltpu.get_barrier_semaphore()
    partners = [right, left, other, x_right, x_left]
    for dy in range(1, NY):
        for c2 in range(NC):
            partners.append(at(lax.rem(y + dy, NY), z, c2))
    for dev in partners:
        pl.semaphore_signal(barrier, inc=1, device_id=dev, device_id_type=MESH)
    for copy in loads:
        copy.wait()
    pl.semaphore_wait(barrier, len(partners))

    def z_copies(p, k):
        if k < 4:
            a = remote(zs[p][(9 - k) % 8], zs[p][8 - k], zsend.at[p, k - 1, 0], zrecv.at[p, k - 1, 0], right)
            b = remote(zs[p][k - 1], zs[p][k], zsend.at[p, k - 1, 1], zrecv.at[p, k - 1, 1], left)
        else:
            lo, hi = pl.ds(0, blocks // 2), pl.ds(blocks // 2, blocks - blocks // 2)
            a = remote(zs[p][5].at[lo], zs[p][4].at[lo], zsend.at[p, 3, 0], zrecv.at[p, 3, 0], right)
            b = remote(zs[p][3].at[hi], zs[p][4].at[hi], zsend.at[p, 3, 1], zrecv.at[p, 3, 1], left)
        return a, b

    def z_start(p, k):
        for copy in z_copies(p, k):
            copy.start()

    def z_wait(p, k):
        for copy in z_copies(p, k):
            copy.wait_recv()

    z_start(0, 1)

    def table(g_there, sem, dev):
        return remote(want_ref, tabs.at[g_there], tsend.at[sem], trecv.at[g_there], dev)

    def table_in(g):
        return pltpu.make_async_copy(tabs.at[g], tabs_smem.at[g], tab_local.at[g])

    table(0, 0, other).start()
    for dy in range(1, NY):
        @pl.when(y >= dy)
        def _():
            for c2 in range(NC):
                table(2 * dy - 1 + c, 2 * dy - 1 + c2, at(y - dy, z, c2)).start()
    table(0, 0, other).wait_recv()
    table_in(0).start()
    for dy in range(1, NY):
        @pl.when(y + dy < NY)
        def _():
            for c2 in range(NC):
                g = 2 * dy - 1 + c2
                table(g, g, other).wait_recv()
                table_in(g).start()
    table_in(0).wait()
    for dy in range(1, NY):
        @pl.when(y + dy < NY)
        def _():
            for c2 in range(NC):
                table_in(2 * dy - 1 + c2).wait()

    def y_copy(p, g_here, g_there, place, dev):
        return remote(
            sp[p].at[pl.ds(g_here * SPAN + place[0], place[1])],
            rp[p].at[pl.ds(g_there * SPAN + place[0], place[1])],
            ysend.at[p, g_here], yrecv.at[p, g_there], dev,
        )

    starts = (0, 1, 3, 5, 7)

    def owner_at(d):
        return (y * NZ + lax.rem(z + d, NZ)) * NC + c

    def push(p, k):
        place = (starts[k], len(ARRIVAL[k]))

        def pack(g):
            for j, d in enumerate(ARRIVAL[k]):
                sp[p][g * SPAN + place[0] + j] = zs[p][d][tabs_smem[g, 0, owner_at(d)]]

        for dy in (2, 1, 3):
            @pl.when(y + dy < NY)
            def _():
                for c2 in range(NC):
                    g = 2 * dy - 1 + c2
                    pack(g)
                    y_copy(p, g, 2 * dy - 1 + c, place, at(y + dy, z, c2)).start()
        pack(0)
        y_copy(p, 0, 0, place, other).start()
        for j, d in enumerate(ARRIVAL[k]):
            rp[p][7 * SPAN + place[0] + j] = zs[p][d][want_smem[0, owner_at(d)]]
        for d in ARRIVAL[k]:
            @pl.when((y == 0) & (c == 0) & (z == (8 - d) % 8))
            def _():
                zero[p][...] = zs[p][d][0]

    def n_copy(p, g_there, sem, dev):
        return remote(zero[p], rp[p].at[g_there * SPAN + 8], nsend.at[p, sem], nrecv.at[p], dev)

    def push_zero(p):
        @pl.when((y == 0) & (c == 0))
        def _():
            for dy in range(1, NY):
                for c2 in range(NC):
                    g = 2 * dy - 1 + c2
                    n_copy(p, 2 * dy - 1, g, at(dy, z, c2)).start()
            n_copy(p, 0, 0, other).start()
            rp[p][7 * SPAN + 8] = zero[p][...]

    def y_wait(p):
        whole = (0, 8)
        y_copy(p, 0, 0, whole, other).wait_recv()
        for dy in range(1, NY):
            @pl.when(y >= dy)
            def _():
                for c2 in range(NC):
                    g = 2 * dy - 1 + c2
                    y_copy(p, g, g, whole, other).wait_recv()
                    if c2 == 0:
                        @pl.when(y == dy)
                        def _():
                            n_copy(p, g, g, other).wait_recv()
        @pl.when((y == 0) & (c == 1))
        def _():
            n_copy(p, 0, 0, other).wait_recv()

    cut = (slots + 1) // 2
    first, second = pl.ds(0, cut), pl.ds(cut, slots - cut)

    def compact(p):
        zero_group = jnp.where(y == 0, jnp.where(c == 0, 7, 0), 2 * y - 1)
        xs[p][0] = rp[p][zero_group * SPAN + 8]
        for j in range(slots - 1):
            xs[p][j + 1] = rp[p][source_ref[j]]

    def quarter(of):
        return pl.ds(pl.multiple_of(of * rows, rows), rows)

    def x_direct(p, part, way):
        sem = 2 * way + part
        span = (first, second)[part]
        return remote(
            xs[p].at[span], outs[p].at[span, mine, :],
            xsend.at[p, sem], xrecv.at[p, sem], (x_right, x_left)[way],
        )

    def x_direct_in(p, part, way):
        sem = 2 * way + part
        span = (first, second)[part]
        return remote(
            xs[p].at[span], outs[p].at[span, quarter((xl, xr)[way]), :],
            xsend.at[p, sem], xrecv.at[p, sem], (x_right, x_left)[way],
        )

    def x_relay(p, way):
        span = (first, second)[way]
        region = outs[p].at[span, quarter((xl, xr)[way]), :]
        return remote(region, region, xsend.at[p, 4 + way], xrecv.at[p, 4 + way], (x_right, x_left)[way])

    def x_relay_in(p, way):
        span = (first, second)[way]
        region = outs[p].at[span, quarter(lax.rem(x + 2, NX)), :]
        return remote(region, region, xsend.at[p, 4 + way], xrecv.at[p, 4 + way], (x_right, x_left)[way])

    def x_own(p):
        return pltpu.make_async_copy(xs[p], outs[p].at[:, mine, :], xlocal.at[p])

    def x_start(p):
        x_direct(p, 0, 0).start()
        x_direct(p, 1, 1).start()
        x_direct(p, 1, 0).start()
        x_direct(p, 0, 1).start()
        x_own(p).start()

    def x_forward(p):
        x_direct_in(p, 0, 0).wait_recv()
        x_relay(p, 0).start()
        x_direct_in(p, 1, 1).wait_recv()
        x_relay(p, 1).start()

    def x_finish(p):
        x_direct_in(p, 1, 0).wait_recv()
        x_direct_in(p, 0, 1).wait_recv()
        x_relay_in(p, 0).wait_recv()
        x_relay_in(p, 1).wait_recv()
        x_own(p).wait()

    push(0, 0)
    for k in range(1, 5):
        z_wait(0, k)
        if k < 4:
            z_start(0, k + 1)
        else:
            z_start(1, 1)
        push(0, k)
    push_zero(0)
    push(1, 0)
    z_wait(1, 1)
    z_start(1, 2)
    push(1, 1)
    y_wait(0)
    compact(0)
    x_start(0)
    z_wait(1, 2)
    z_start(1, 3)
    push(1, 2)
    z_wait(1, 3)
    z_start(1, 4)
    push(1, 3)
    x_forward(0)
    z_wait(1, 4)
    push(1, 4)
    push_zero(1)
    y_wait(1)
    compact(1)
    x_start(1)
    x_finish(0)
    x_forward(1)
    x_finish(1)

    for p in range(2):
        for k in range(1, 5):
            for copy in z_copies(p, k):
                copy.wait_send()
        whole = (0, 8)
        y_copy(p, 0, 0, whole, other).wait_send()
        for dy in range(1, NY):
            @pl.when(y + dy < NY)
            def _():
                for c2 in range(NC):
                    g = 2 * dy - 1 + c2
                    y_copy(p, g, g, whole, other).wait_send()
        @pl.when((y == 0) & (c == 0))
        def _():
            for g in range(7):
                n_copy(p, 0, g, other).wait_send()
        for part in range(2):
            for way in range(2):
                x_direct(p, part, way).wait_send()
        for way in range(2):
            x_relay(p, way).wait_send()
    table(0, 0, other).wait_send()
    for dy in range(1, NY):
        @pl.when(y >= dy)
        def _():
            for c2 in range(NC):
                table(0, 2 * dy - 1 + c2, other).wait_send()


def attend(blocks, slots, tile_ref, q_ref, k_hbm, v_hbm, gk_hbm, gv_hbm, out_ref, kt, vt, sc, sem):
    block_len, width = q_ref.shape
    head = kt.shape[-1]
    null = blocks + slots
    step = pl.program_id(0)

    @pl.when(step == 0)
    def _():
        copies = [
            pltpu.make_async_copy(k_hbm, kt.at[pl.ds(0, blocks)], sem.at[0]),
            pltpu.make_async_copy(v_hbm, vt.at[pl.ds(0, blocks), :, pl.ds(0, head)], sem.at[1]),
            pltpu.make_async_copy(gk_hbm, kt.at[pl.ds(blocks, slots)], sem.at[2]),
            pltpu.make_async_copy(gv_hbm, vt.at[pl.ds(blocks, slots), :, pl.ds(0, head)], sem.at[3]),
        ]
        for copy in copies:
            copy.start()
        for t in range(null):
            vt[t, :, head:] = jnp.ones((block_len, head), jnp.bfloat16)
        vt[null] = jnp.zeros((block_len, 2 * head), jnp.bfloat16)
        for copy in copies:
            copy.wait()
        kt[null] = jnp.broadcast_to(kt[blocks, :1, :], (block_len, head))

    factor = math.log2(math.e) / math.sqrt(head)
    half = block_len // 2
    tiles = [tile_ref[step, j] for j in range(4)]
    for h in range(width // head):
        for r in range(2):
            q = q_ref[pl.ds(r * half, half), pl.ds(h * head, head)]
            own = (r + 1) * half

            def score(keys):
                return lax.dot_general(q, keys, (((1,), (1,)), ((), ())), preferred_element_type=jnp.float32)

            s = score(kt[step, :own])
            row = lax.broadcasted_iota(jnp.int32, (half, own), 0) + r * half
            col = lax.broadcasted_iota(jnp.int32, (half, own), 1)
            s = jnp.where(col <= row, s, -1e30)
            sc[:, :own] = s
            top = jnp.max(s, axis=1, keepdims=True)
            for j in range(4):
                s = score(kt[tiles[j]])
                sc[:, pl.ds((j + 1) * block_len, block_len)] = s
                top = jnp.maximum(top, jnp.max(s, axis=1, keepdims=True))
            shift = top * factor
            p = jnp.exp2(sc[:, :own] * factor - shift).astype(jnp.bfloat16)
            acc = jnp.dot(p, vt[step, :own], preferred_element_type=jnp.float32)
            for j in range(4):
                s = sc[:, pl.ds((j + 1) * block_len, block_len)]
                p = jnp.exp2(s * factor - shift).astype(jnp.bfloat16)
                acc += jnp.dot(p, vt[tiles[j]], preferred_element_type=jnp.float32)
            out = acc[:, :head] / acc[:, head:]
            out_ref[pl.ds(r * half, half), pl.ds(h * head, head)] = out.astype(jnp.bfloat16)


def shards(queries, keys, values, selected):
    me = lax.axis_index("seq")
    blocks, per_block = selected.shape
    head = keys.shape[1]
    block_len = keys.shape[0] // blocks
    rows = block_len // NX
    slots = blocks * per_block + 1
    k3 = keys.reshape(blocks, block_len, head)
    v3 = values.reshape(blocks, block_len, head)

    owner = (selected // blocks).reshape(-1)
    local = (selected % blocks).reshape(-1)
    remote = owner != me
    hits = (owner[:, None] == jnp.arange(128, dtype=jnp.int32)[None, :]) & remote[:, None]
    want = jnp.sum(jnp.where(hits, local[:, None], 0), axis=0).astype(jnp.int32)
    want = jnp.broadcast_to(want[None, :], (8, 128))
    y, z, c = me // (NZ * NC), (me // NC) % NZ, me % NC
    oy, oz, oc = owner // (NZ * NC), (owner // NC) % NZ, owner % NC
    dy, dz = y - oy, (oz - z) % NZ
    group = jnp.where(dy == 0, jnp.where(oc == c, 7, 0), 2 * dy - 1 + oc)
    place = jnp.where(dz <= 4, jnp.where(dz == 4, 7, 2 * dz), 2 * (NZ - dz) - 1)
    live = live_slots(selected).reshape(-1)
    source = jnp.where(live & remote, group * SPAN + place, 7 * SPAN).astype(jnp.int32)

    part = lambda *shape: pltpu.VMEM(shape + (rows, head), jnp.bfloat16)
    smem = pl.BlockSpec(memory_space=pltpu.SMEM)
    hbm = pl.BlockSpec(memory_space=pl.ANY)
    dma = pltpu.SemaphoreType.DMA
    got = jax.ShapeDtypeStruct((slots, block_len, head), jnp.bfloat16)
    gk, gv = pl.pallas_call(
        functools.partial(exchange, blocks, rows, slots),
        out_shape=(got, got),
        in_specs=[smem, smem, pl.BlockSpec(memory_space=pltpu.VMEM), hbm, hbm],
        out_specs=(hbm, hbm),
        scratch_shapes=[part(blocks)] * 16
        + [part(7 * SPAN)] * 2
        + [part(GROUPS * SPAN)] * 2
        + [part()] * 2
        + [part(slots)] * 2
        + [
            pltpu.VMEM((7, 8, 128), jnp.int32), pltpu.SMEM((7, 8, 128), jnp.int32),
            dma((2,)), dma((7,)),
            dma((2, 4, 2)), dma((2, 4, 2)), dma((2, 7)), dma((2, 7)), dma((2, 7)), dma((2,)),
            dma((7,)), dma((7,)), dma((2, 6)), dma((2, 6)), dma((2,)),
        ],
        compiler_params=pltpu.CompilerParams(
            collective_id=0, has_side_effects=True, vmem_limit_bytes=40 * 2**20
        ),
    )(source, want, want, k3, v3)

    numbers = me * blocks + jnp.arange(blocks, dtype=jnp.int32)
    null = blocks + slots
    tile = jnp.where(remote, blocks + 1 + jnp.arange(blocks * per_block, dtype=jnp.int32), local)
    tile = jnp.where(live, tile, null).reshape(blocks, per_block)
    front = jnp.where(numbers != 0, blocks, null)
    tiles = jnp.concatenate([front[:, None], tile], axis=1).astype(jnp.int32)

    return pl.pallas_call(
        functools.partial(attend, blocks, slots),
        out_shape=jax.ShapeDtypeStruct(queries.shape, jnp.bfloat16),
        grid_spec=pltpu.PrefetchScalarGridSpec(
            num_scalar_prefetch=1,
            grid=(blocks,),
            in_specs=[pl.BlockSpec((block_len, queries.shape[1]), lambda i, t: (i, 0)), hbm, hbm, hbm, hbm],
            out_specs=pl.BlockSpec((block_len, queries.shape[1]), lambda i, t: (i, 0)),
            scratch_shapes=[
                pltpu.VMEM((null + 1, block_len, head), jnp.bfloat16),
                pltpu.VMEM((null + 1, block_len, 2 * head), jnp.bfloat16),
                pltpu.VMEM((block_len // 2, 5 * block_len), jnp.float32),
                dma((4,)),
            ],
        ),
        compiler_params=pltpu.CompilerParams(vmem_limit_bytes=40 * 2**20),
    )(tiles, queries, k3, v3, gk, gv)


def solution(mesh):
    in_specs = (P("seq", "head"), P("seq", None), P("seq", None), P("seq", None))
    return jax.shard_map(shards, mesh=mesh, in_specs=in_specs, out_specs=P("seq", "head"), check_vma=False)
```

```python
import functools
import math

import jax
import jax.numpy as jnp
from jax import lax
from jax.experimental import pallas as pl
from jax.experimental.pallas import tpu as pltpu
from jax.sharding import PartitionSpec as P

MESH = pl.DeviceIdType.MESH
NY, NZ, NC, NX = 4, 8, 2, 4
GROUPS = 8
SPAN = 9
ARRIVAL = ((0,), (7, 1), (6, 2), (5, 3), (4,))
STARTS = (0, 1, 3, 5, 7)
PARTS = 4


def fused(blocks, picks, block_len, heads, sel, q_hbm, k_hbm, v_hbm, out_hbm, *scratch):
    rows = block_len // (2 * NX)
    half = block_len // 2
    head = k_hbm.shape[-1]
    slots = blocks * picks + 1
    null = blocks + slots
    zs = [scratch[8 * p:8 * p + 8] for p in range(PARTS)]
    sp = scratch[32:36]
    rp = scratch[36:40]
    zero = scratch[40:44]
    tiles = scratch[44:48]
    (q_vm, k_vm, v_vm, out_vm, prob, sc, m_ref, l_ref, acc_ref, want_ref,
     tabs, tabs_smem, load_sem, tab_local, zsend, zrecv, ysend, yrecv, nsend, nrecv,
     tsend, trecv, xsend, xrecv, out_sem) = scratch[48:]
    s = lax.axis_index("seq")
    x = lax.axis_index("head")
    c = lax.rem(s, NC)
    z = lax.rem(s // NC, NZ)
    y = s // (NC * NZ)

    def at(y2, z2, c2):
        return ((y2 * NZ + z2) * NC + c2, x)

    zr, zl = lax.rem(z + 1, NZ), lax.rem(z + NZ - 1, NZ)
    xr, xl, xo = lax.rem(x + 1, NX), lax.rem(x + NX - 1, NX), lax.rem(x + 2, NX)
    right, left = at(y, zr, c), at(y, zl, c)
    other = at(y, z, 1 - c)
    x_right, x_left = (s, xr), (s, xl)

    def remote(src, dst, ss, rs, dev):
        return pltpu.make_async_remote_copy(
            src_ref=src, dst_ref=dst, send_sem=ss, recv_sem=rs, device_id=dev, device_id_type=MESH
        )

    def source(p):
        return (k_hbm, v_hbm)[p % 2]

    loads = [pltpu.make_async_copy(source(p).at[:, x, p // 2], zs[p][0], load_sem.at[p]) for p in range(PARTS)]
    for p in range(PARTS):
        loads.append(
            pltpu.make_async_copy(
                source(p).at[:, :, p // 2], tiles[p].at[pl.ds(0, blocks)], load_sem.at[PARTS + p]
            )
        )
    loads.append(pltpu.make_async_copy(k_hbm, k_vm, load_sem.at[8]))
    loads.append(pltpu.make_async_copy(v_hbm, v_vm, load_sem.at[9]))
    loads.append(pltpu.make_async_copy(q_hbm, q_vm, load_sem.at[10]))
    for copy in loads:
        copy.start()

    barrier = pltpu.get_barrier_semaphore()
    partners = [right, left, other, x_right, x_left]
    for dy in range(1, NY):
        for c2 in range(NC):
            partners.append(at(lax.rem(y + dy, NY), z, c2))
    for dev in partners:
        pl.semaphore_signal(barrier, inc=1, device_id=dev, device_id_type=MESH)

    lane = lax.broadcasted_iota(jnp.int32, (8, 128), 1)
    want = jnp.zeros((8, 128), jnp.int32)
    for b in range(blocks):
        for j in range(picks):
            chosen = sel[b, j]
            owner = jnp.where(chosen != 0, chosen // blocks, -1)
            want = jnp.where(lane == owner, lax.rem(chosen, blocks), want)
    want_ref[...] = jnp.where(lane == s, 0, want)
    own_table = pltpu.make_async_copy(want_ref, tabs_smem.at[7], tab_local.at[7])
    own_table.start()

    def live(b, j):
        chosen = sel[b, j]
        ok = chosen != 0
        for i in range(j):
            ok = ok & (chosen != sel[b, i])
        return ok

    def slot_source(b, j):
        owner = sel[b, j] // blocks
        oy, oz, oc = owner // (NZ * NC), lax.rem(owner // NC, NZ), lax.rem(owner, NC)
        dy, dz = y - oy, lax.rem(oz - z + NZ, NZ)
        group = jnp.where(dy == 0, jnp.where(oc == c, 7, 0), 2 * dy - 1 + oc)
        place = jnp.where(dz < 4, 2 * dz, jnp.where(dz == 4, 7, 2 * (NZ - dz) - 1))
        return jnp.where(live(b, j) & (owner != s), group * SPAN + place, 7 * SPAN)

    def tile_of(b, j):
        if j == 0:
            return jnp.where(s * blocks + b != 0, blocks, null)
        chosen = sel[b, j - 1]
        here = jnp.where(chosen // blocks == s, lax.rem(chosen, blocks), blocks + 1 + b * picks + (j - 1))
        return jnp.where(live(b, j - 1), here, null)

    for copy in loads[:PARTS]:
        copy.wait()
    pl.semaphore_wait(barrier, len(partners))

    def z_copies(p, k):
        if k < 4:
            a = remote(zs[p][(9 - k) % 8], zs[p][8 - k], zsend.at[p, k - 1, 0], zrecv.at[p, k - 1, 0], right)
            b = remote(zs[p][k - 1], zs[p][k], zsend.at[p, k - 1, 1], zrecv.at[p, k - 1, 1], left)
        else:
            lo, hi = pl.ds(0, blocks // 2), pl.ds(blocks // 2, blocks - blocks // 2)
            a = remote(zs[p][5].at[lo], zs[p][4].at[lo], zsend.at[p, 3, 0], zrecv.at[p, 3, 0], right)
            b = remote(zs[p][3].at[hi], zs[p][4].at[hi], zsend.at[p, 3, 1], zrecv.at[p, 3, 1], left)
        return a, b

    def z_start(p, k):
        for copy in z_copies(p, k):
            copy.start()

    def z_wait(p, k):
        for copy in z_copies(p, k):
            copy.wait_recv()

    z_start(0, 1)

    def table(g_there, sem, dev):
        return remote(want_ref, tabs.at[g_there], tsend.at[sem], trecv.at[g_there], dev)

    def table_in(g):
        return pltpu.make_async_copy(tabs.at[g], tabs_smem.at[g], tab_local.at[g])

    table(0, 0, other).start()
    for dy in range(1, NY):
        @pl.when(y >= dy)
        def _():
            for c2 in range(NC):
                table(2 * dy - 1 + c, 2 * dy - 1 + c2, at(y - dy, z, c2)).start()
    table(0, 0, other).wait_recv()
    table_in(0).start()
    for dy in range(1, NY):
        @pl.when(y + dy < NY)
        def _():
            for c2 in range(NC):
                g = 2 * dy - 1 + c2
                table(g, g, other).wait_recv()
                table_in(g).start()
    table_in(0).wait()
    for dy in range(1, NY):
        @pl.when(y + dy < NY)
        def _():
            for c2 in range(NC):
                table_in(2 * dy - 1 + c2).wait()
    own_table.wait()

    def y_copy(p, g_here, g_there, place, dev):
        return remote(
            sp[p].at[pl.ds(g_here * SPAN + place[0], place[1])],
            rp[p].at[pl.ds(g_there * SPAN + place[0], place[1])],
            ysend.at[p, g_here], yrecv.at[p, g_there], dev,
        )

    def owner_at(d):
        return (y * NZ + lax.rem(z + d, NZ)) * NC + c

    def push(p, k):
        place = (STARTS[k], len(ARRIVAL[k]))

        def pack(g):
            for j, d in enumerate(ARRIVAL[k]):
                sp[p][g * SPAN + place[0] + j] = zs[p][d][tabs_smem[g, 0, owner_at(d)]]

        for dy in (2, 1, 3):
            @pl.when(y + dy < NY)
            def _():
                for c2 in range(NC):
                    g = 2 * dy - 1 + c2
                    pack(g)
                    y_copy(p, g, 2 * dy - 1 + c, place, at(y + dy, z, c2)).start()
        pack(0)
        y_copy(p, 0, 0, place, other).start()
        for j, d in enumerate(ARRIVAL[k]):
            rp[p][7 * SPAN + place[0] + j] = zs[p][d][tabs_smem[7, 0, owner_at(d)]]
        for d in ARRIVAL[k]:
            @pl.when((y == 0) & (c == 0) & (z == (8 - d) % 8))
            def _():
                zero[p][...] = zs[p][d][0]
        if k == 4:
            push_zero(p)

    def n_copy(p, g_there, sem, dev):
        return remote(zero[p], rp[p].at[g_there * SPAN + 8], nsend.at[p, sem], nrecv.at[p], dev)

    def push_zero(p):
        @pl.when((y == 0) & (c == 0))
        def _():
            for dy in range(1, NY):
                for c2 in range(NC):
                    g = 2 * dy - 1 + c2
                    n_copy(p, 2 * dy - 1, g, at(dy, z, c2)).start()
            n_copy(p, 0, 0, other).start()
            rp[p][7 * SPAN + 8] = zero[p][...]

    def y_wait(p):
        whole = (0, 8)
        y_copy(p, 0, 0, whole, other).wait_recv()
        for dy in range(1, NY):
            @pl.when(y >= dy)
            def _():
                for c2 in range(NC):
                    g = 2 * dy - 1 + c2
                    y_copy(p, g, g, whole, other).wait_recv()
                    if c2 == 0:
                        @pl.when(y == dy)
                        def _():
                            n_copy(p, g, g, other).wait_recv()
        @pl.when((y == 0) & (c == 1))
        def _():
            n_copy(p, 0, 0, other).wait_recv()

    cut = (slots + 1) // 2
    spans = (pl.ds(blocks, cut), pl.ds(blocks + cut, slots - cut))

    def compact(p):
        zero_group = jnp.where(y == 0, jnp.where(c == 0, 7, 0), 2 * y - 1)
        tiles[p][blocks, x] = rp[p][zero_group * SPAN + 8]
        for b in range(blocks):
            for j in range(picks):
                tiles[p][blocks + 1 + b * picks + j, x] = rp[p][slot_source(b, j)]

    def x_copy(p, span, of, sem, way):
        region = tiles[p].at[spans[span], of]
        return remote(region, region, xsend.at[p, sem], xrecv.at[p, sem], (x_right, x_left)[way])

    def x_start(p):
        x_copy(p, 0, x, 0, 0).start()
        x_copy(p, 1, x, 3, 1).start()
        x_copy(p, 1, x, 1, 0).start()
        x_copy(p, 0, x, 2, 1).start()

    def x_forward(p):
        x_copy(p, 0, xl, 0, 0).wait_recv()
        x_copy(p, 0, xl, 4, 0).start()
        x_copy(p, 1, xr, 3, 1).wait_recv()
        x_copy(p, 1, xr, 5, 1).start()

    def x_finish(p):
        x_copy(p, 1, xl, 1, 0).wait_recv()
        x_copy(p, 0, xr, 2, 1).wait_recv()
        x_copy(p, 0, xo, 4, 0).wait_recv()
        x_copy(p, 1, xo, 5, 1).wait_recv()

    def step(p, k):
        y_wait(p)
        compact(p)
        x_start(p)

    factor = math.log2(math.e) / math.sqrt(head)
    lanes = 128

    def score(q, keys):
        return lax.dot_general(q, keys, (((1,), (1,)), ((), ())), preferred_element_type=jnp.float32)

    def chunks(b):
        for h in range(heads):
            for r in range(2):
                start = pl.multiple_of(b * block_len, block_len) + r * half
                yield (b * heads + h) * 2 + r, r, pl.ds(start, half), pl.ds(h * head, head)

    def own_part(b0, b1):
        def body(b, _):
            for i, r, at_rows, at_head in chunks(b):
                own = (r + 1) * half
                t = score(q_vm[at_rows, at_head], k_vm[b].reshape(block_len, head)[:own])
                row = lax.broadcasted_iota(jnp.int32, (half, own), 0) + r * half
                col = lax.broadcasted_iota(jnp.int32, (half, own), 1)
                t = jnp.where(col <= row, t, -1e30)
                top = jnp.broadcast_to(jnp.max(t, axis=1, keepdims=True), (half, lanes))
                m_ref[i] = top
                shift = top * factor
                total = jnp.zeros((half, lanes), jnp.float32)
                out = jnp.zeros((half, head), jnp.float32)
                ps = []
                for n in range(own // lanes):
                    e = jnp.exp2(t[:, n * lanes:(n + 1) * lanes] * factor - shift)
                    total += e
                    ps.append(e.astype(jnp.bfloat16))
                l_ref[i] = total
                acc_ref[i] = jnp.dot(
                    jnp.concatenate(ps, axis=1),
                    v_vm[b].reshape(block_len, head)[:own],
                    preferred_element_type=jnp.float32,
                )
            return 0

        lax.fori_loop(b0, b1, body, 0)

    def soft_part(p, b0, b1, last):
        def body(b, _):
            picked = [tile_of(b, j) for j in range(picks + 1)]
            for i, r, at_rows, at_head in chunks(b):
                q = q_vm[at_rows, at_head]
                top = m_ref[i]
                old = top
                for j in range(picks + 1):
                    t = score(q, tiles[p][picked[j]].reshape(half, head))
                    sc[:, pl.ds(j * half, half)] = t
                    top = jnp.maximum(top, jnp.max(t, axis=1, keepdims=True))
                shift = top * factor
                scale = jnp.exp2(old * factor - shift)
                total = l_ref[i] * scale
                for j in range(picks + 1):
                    part = jnp.zeros((half, lanes), jnp.float32)
                    for n in range(j * half // lanes, (j + 1) * half // lanes):
                        e = jnp.exp2(sc[:, pl.ds(n * lanes, lanes)] * factor - shift)
                        part += e
                        prob[i, :, pl.ds(n * lanes, lanes)] = e.astype(jnp.bfloat16)
                    total += part * jnp.where(picked[j] == null, 0.0, 1.0)
                if last:
                    full = jnp.sum(total, axis=1, keepdims=True)
                    total = jnp.broadcast_to(1.0 / full, (half, lanes))
                l_ref[i] = total
                m_ref[i] = top
                acc_ref[i] = acc_ref[i] * scale
            return 0

        lax.fori_loop(b0, b1, body, 0)

    def out_copy(b):
        at_rows = pl.ds(pl.multiple_of(b * block_len, block_len), block_len)
        return pltpu.make_async_copy(out_vm.at[at_rows], out_hbm.at[at_rows], out_sem.at[b])

    def value_part(p, b0, b1, last):
        def body(b, _):
            picked = [tile_of(b, j) for j in range(picks + 1)]
            for i, r, at_rows, at_head in chunks(b):
                out = acc_ref[i]
                for j in range(picks + 1):
                    out += jnp.dot(
                        prob[i, :, pl.ds(j * half, half)],
                        tiles[p][picked[j]].reshape(half, head),
                        preferred_element_type=jnp.float32,
                    )
                if last:
                    out_vm[at_rows, at_head] = (out * l_ref[i]).astype(jnp.bfloat16)
                else:
                    acc_ref[i] = out
            if last:
                out_copy(b).start()
            return 0

        lax.fori_loop(b0, b1, body, 0)

    push(0, 0)
    z_start(1, 1)
    for copy in loads[PARTS:]:
        copy.wait()
    own_part(0, 2)
    z_wait(0, 1)
    z_start(0, 2)
    push(0, 1)
    push(1, 0)
    z_wait(0, 2)
    z_start(0, 3)
    push(0, 2)
    z_wait(1, 1)
    z_start(1, 2)
    own_part(2, 4)
    z_wait(0, 3)
    z_start(0, 4)
    push(0, 3)
    z_wait(1, 2)
    z_start(1, 3)
    z_wait(0, 4)
    push(0, 4)
    push(1, 1)
    push(1, 2)
    z_start(2, 1)
    z_wait(1, 3)
    z_start(1, 4)
    push(1, 3)
    push(2, 0)
    own_part(4, 6)
    z_wait(2, 1)
    z_start(2, 2)
    z_wait(1, 4)
    push(1, 4)
    z_start(3, 1)
    y_wait(0)
    compact(0)
    x_start(0)
    z_wait(2, 2)
    z_start(2, 3)
    push(2, 1)
    push(2, 2)
    z_wait(3, 1)
    z_start(3, 2)
    z_wait(2, 3)
    z_start(2, 4)
    push(2, 3)
    push(3, 0)
    x_forward(0)
    z_wait(3, 2)
    z_start(3, 3)
    z_wait(2, 4)
    push(2, 4)
    push(3, 1)
    push(3, 2)
    y_wait(1)
    compact(1)
    x_start(1)
    z_wait(3, 3)
    z_start(3, 4)
    push(3, 3)
    x_finish(0)
    first_key = jnp.broadcast_to(tiles[0][blocks, 0, :1, :].reshape(1, 1, head), (NX, rows, head))
    tiles[0][null] = first_key
    tiles[2][null] = first_key
    tiles[1][null] = jnp.zeros((NX, rows, head), jnp.bfloat16)
    tiles[3][null] = jnp.zeros((NX, rows, head), jnp.bfloat16)
    soft_part(0, 0, 2, False)
    z_wait(3, 4)
    push(3, 4)
    x_forward(1)
    soft_part(0, 2, 6, False)
    y_wait(2)
    compact(2)
    x_start(2)
    x_finish(1)
    value_part(1, 0, 3, False)
    x_forward(2)
    value_part(1, 3, 6, False)
    y_wait(3)
    compact(3)
    x_start(3)
    x_finish(2)
    soft_part(2, 0, 2, True)
    x_forward(3)
    soft_part(2, 2, 6, True)
    x_finish(3)
    value_part(3, 0, 6, True)

    for p in range(PARTS):
        for k in range(1, 5):
            for copy in z_copies(p, k):
                copy.wait_send()
        whole = (0, 8)
        y_copy(p, 0, 0, whole, other).wait_send()
        for dy in range(1, NY):
            @pl.when(y + dy < NY)
            def _():
                for c2 in range(NC):
                    g = 2 * dy - 1 + c2
                    y_copy(p, g, g, whole, other).wait_send()
        @pl.when((y == 0) & (c == 0))
        def _():
            for g in range(7):
                n_copy(p, 0, g, other).wait_send()
        x_copy(p, 0, x, 0, 0).wait_send()
        x_copy(p, 1, x, 3, 1).wait_send()
        x_copy(p, 1, x, 1, 0).wait_send()
        x_copy(p, 0, x, 2, 1).wait_send()
        x_copy(p, 0, xl, 4, 0).wait_send()
        x_copy(p, 1, xr, 5, 1).wait_send()
    table(0, 0, other).wait_send()
    for dy in range(1, NY):
        @pl.when(y >= dy)
        def _():
            for c2 in range(NC):
                table(0, 2 * dy - 1 + c2, other).wait_send()
    for b in range(blocks):
        out_copy(b).wait()


def shards(queries, keys, values, selected):
    blocks, picks = selected.shape
    head = keys.shape[1]
    block_len = keys.shape[0] // blocks
    heads = queries.shape[1] // head
    rows = block_len // (2 * NX)
    half = block_len // 2
    slots = blocks * picks + 1
    k5 = keys.reshape(blocks, NX, 2, rows, head)
    v5 = values.reshape(blocks, NX, 2, rows, head)
    part = lambda *shape: pltpu.VMEM(shape + (rows, head), jnp.bfloat16)
    wide = lambda *shape: pltpu.VMEM(shape, jnp.float32)
    hbm = pl.BlockSpec(memory_space=pl.ANY)
    dma = pltpu.SemaphoreType.DMA
    chunks = blocks * heads * 2
    return pl.pallas_call(
        functools.partial(fused, blocks, picks, block_len, heads),
        out_shape=jax.ShapeDtypeStruct(queries.shape, jnp.bfloat16),
        in_specs=[pl.BlockSpec(memory_space=pltpu.SMEM), hbm, hbm, hbm],
        out_specs=hbm,
        scratch_shapes=[part(blocks)] * 32
        + [part(7 * SPAN)] * 4
        + [part(GROUPS * SPAN)] * 4
        + [part()] * 4
        + [part(blocks + slots + 1, NX)] * 4
        + [
            pltpu.VMEM(queries.shape, jnp.bfloat16),
            part(blocks, NX, 2), part(blocks, NX, 2),
            pltpu.VMEM(queries.shape, jnp.bfloat16),
            pltpu.VMEM((chunks, half, (picks + 1) * half), jnp.bfloat16),
            wide(half, (picks + 1) * half),
            wide(chunks, half, 128), wide(chunks, half, 128), wide(chunks, half, head),
            pltpu.VMEM((8, 128), jnp.int32),
            pltpu.VMEM((7, 8, 128), jnp.int32), pltpu.SMEM((8, 8, 128), jnp.int32),
            dma((11,)), dma((8,)),
            dma((4, 4, 2)), dma((4, 4, 2)), dma((4, 7)), dma((4, 7)), dma((4, 7)), dma((4,)),
            dma((7,)), dma((7,)), dma((4, 6)), dma((4, 6)), dma((blocks,)),
        ],
        compiler_params=pltpu.CompilerParams(
            collective_id=0, has_side_effects=True, vmem_limit_bytes=56 * 2**20
        ),
    )(selected, queries, k5, v5)


def solution(mesh):
    in_specs = (P("seq", "head"), P("seq", None), P("seq", None), P("seq", None))
    return jax.shard_map(shards, mesh=mesh, in_specs=in_specs, out_specs=P("seq", "head"), check_vma=False)
```

```python
import functools
import math

import jax
import jax.numpy as jnp
from jax import lax
from jax.experimental import pallas as pl
from jax.experimental.pallas import tpu as pltpu
from jax.sharding import PartitionSpec as P

MESH = pl.DeviceIdType.MESH
NY, NZ, NC, NX = 4, 8, 2, 4
GROUPS = 8
SPAN = 9
ARRIVAL = ((0, 7, 1), (6, 2), (5, 3, 4))
STARTS = (0, 3, 5)
SETS = 2
PARTS = 2 * SETS


def fused(blocks, picks, block_len, heads, sel, q_hbm, k_hbm, v_hbm, out_hbm, *scratch):
    rows = block_len // (SETS * NX)
    half = block_len // 2
    head = k_hbm.shape[-1]
    slots = blocks * picks + 1
    null = blocks + slots
    scratch = list(scratch)
    take = lambda n: [scratch.pop(0) for _ in range(n)]
    zs = [take(NZ) for _ in range(PARTS)]
    sp, rp, zero, tiles = take(PARTS), take(PARTS), take(PARTS), take(PARTS)
    (q_vm, k_vm, v_vm, out_vm, prob, sc, m_ref, l_ref, acc_ref, scale_ref, want_ref,
     tabs, tabs_smem, load_sem, tab_local, zsend, zrecv, ysend, yrecv, nsend, nrecv,
     tsend, trecv, xsend, xrecv, out_sem) = scratch
    s = lax.axis_index("seq")
    x = lax.axis_index("head")
    c = lax.rem(s, NC)
    z = lax.rem(s // NC, NZ)
    y = s // (NC * NZ)

    def at(y2, z2, c2):
        return ((y2 * NZ + z2) * NC + c2, x)

    zr, zl = lax.rem(z + 1, NZ), lax.rem(z + NZ - 1, NZ)
    xr, xl, xo = lax.rem(x + 1, NX), lax.rem(x + NX - 1, NX), lax.rem(x + 2, NX)
    right, left = at(y, zr, c), at(y, zl, c)
    other = at(y, z, 1 - c)
    x_right, x_left = (s, xr), (s, xl)

    def remote(src, dst, ss, rs, dev):
        return pltpu.make_async_remote_copy(
            src_ref=src, dst_ref=dst, send_sem=ss, recv_sem=rs, device_id=dev, device_id_type=MESH
        )

    def source(p):
        return (k_hbm, v_hbm)[p % 2]

    loads = [pltpu.make_async_copy(source(p).at[:, x, p // 2], zs[p][0], load_sem.at[p]) for p in range(PARTS)]
    for p in range(PARTS):
        loads.append(
            pltpu.make_async_copy(
                source(p).at[:, :, p // 2], tiles[p].at[pl.ds(0, blocks)], load_sem.at[PARTS + p]
            )
        )
    loads.append(pltpu.make_async_copy(k_hbm, k_vm, load_sem.at[2 * PARTS]))
    loads.append(pltpu.make_async_copy(v_hbm, v_vm, load_sem.at[2 * PARTS + 1]))
    loads.append(pltpu.make_async_copy(q_hbm, q_vm, load_sem.at[2 * PARTS + 2]))
    for copy in loads:
        copy.start()

    lane = lax.broadcasted_iota(jnp.int32, (8, 128), 1)
    want = jnp.zeros((8, 128), jnp.int32)
    for b in range(blocks):
        for j in range(picks):
            chosen = sel[j, b]
            owner = jnp.where(chosen != 0, chosen // blocks, -1)
            want = jnp.where(lane == owner, lax.rem(chosen, blocks), want)
    want_ref[...] = jnp.where(lane == s, 0, want)
    tabs[...] = jnp.where(lane == s, 0, want)

    barrier = pltpu.get_barrier_semaphore()
    partners = [right, left, other, x_right, x_left]
    for dy in range(1, NY):
        for c2 in range(NC):
            partners.append(at(lax.rem(y + dy, NY), z, c2))
    for dev in partners:
        pl.semaphore_signal(barrier, inc=1, device_id=dev, device_id_type=MESH)

    def live(b, j):
        chosen = sel[j, b]
        ok = chosen != 0
        for i in range(j):
            ok = ok & (chosen != sel[i, b])
        return ok

    def slot_source(b, j):
        owner = sel[j, b] // blocks
        oy, oz, oc = owner // (NZ * NC), lax.rem(owner // NC, NZ), lax.rem(owner, NC)
        dy, dz = y - oy, lax.rem(oz - z + NZ, NZ)
        group = jnp.where(dy == 0, jnp.where(oc == c, 7, 0), 2 * dy - 1 + oc)
        place = jnp.where(dz < 4, 2 * dz, jnp.where(dz == 4, 7, 2 * (NZ - dz) - 1))
        return jnp.where(live(b, j) & (owner != s), group * SPAN + place, 7 * SPAN)

    def tile_of(b, j):
        if j == 0:
            return jnp.where(s * blocks + b != 0, blocks, null)
        chosen = sel[j - 1, b]
        here = jnp.where(chosen // blocks == s, lax.rem(chosen, blocks), blocks + 1 + b * picks + (j - 1))
        return jnp.where(live(b, j - 1), here, null)

    for copy in loads[:PARTS]:
        copy.wait()
    pl.semaphore_wait(barrier, len(partners))

    def z_copies(p, k):
        if k < 4:
            a = remote(zs[p][(9 - k) % 8], zs[p][8 - k], zsend.at[p, k - 1, 0], zrecv.at[p, k - 1, 0], right)
            b = remote(zs[p][k - 1], zs[p][k], zsend.at[p, k - 1, 1], zrecv.at[p, k - 1, 1], left)
        else:
            lo, hi = pl.ds(0, blocks // 2), pl.ds(blocks // 2, blocks - blocks // 2)
            a = remote(zs[p][5].at[lo], zs[p][4].at[lo], zsend.at[p, 3, 0], zrecv.at[p, 3, 0], right)
            b = remote(zs[p][3].at[hi], zs[p][4].at[hi], zsend.at[p, 3, 1], zrecv.at[p, 3, 1], left)
        return a, b

    def z_start(p, k):
        for copy in z_copies(p, k):
            copy.start()

    def z_wait(p, k):
        for copy in z_copies(p, k):
            copy.wait_recv()

    z_start(0, 1)

    def table(g_there, sem, dev):
        return remote(want_ref.at[0], tabs.at[g_there], tsend.at[sem], trecv.at[g_there], dev)

    table(0, 0, other).start()
    for dy in range(1, NY):
        @pl.when(y >= dy)
        def _():
            for c2 in range(NC):
                table(2 * dy - 1 + c, 2 * dy - 1 + c2, at(y - dy, z, c2)).start()
    z_start(1, 1)
    table(0, 0, other).wait_recv()
    for dy in range(1, NY):
        @pl.when(y + dy < NY)
        def _():
            for c2 in range(NC):
                g = 2 * dy - 1 + c2
                table(g, g, other).wait_recv()
    tables_in = pltpu.make_async_copy(tabs, tabs_smem, tab_local.at[0])
    tables_in.start()
    tables_in.wait()

    def y_copy(p, g_here, g_there, place, dev):
        return remote(
            sp[p].at[pl.ds(g_here * SPAN + place[0], place[1])],
            rp[p].at[pl.ds(g_there * SPAN + place[0], place[1])],
            ysend.at[p, g_here], yrecv.at[p, g_there], dev,
        )

    def owner_at(d):
        return (y * NZ + lax.rem(z + d, NZ)) * NC + c

    def push(p, k):
        place = (STARTS[k], len(ARRIVAL[k]))

        def pack(g):
            for j, d in enumerate(ARRIVAL[k]):
                sp[p][g * SPAN + place[0] + j] = zs[p][d][tabs_smem[g, owner_at(d)]]

        for dy in (2, 1, 3):
            @pl.when(y + dy < NY)
            def _():
                for c2 in range(NC):
                    g = 2 * dy - 1 + c2
                    pack(g)
                    y_copy(p, g, 2 * dy - 1 + c, place, at(y + dy, z, c2)).start()
        pack(0)
        y_copy(p, 0, 0, place, other).start()
        for j, d in enumerate(ARRIVAL[k]):
            rp[p][7 * SPAN + place[0] + j] = zs[p][d][tabs_smem[7, owner_at(d)]]
        for d in ARRIVAL[k]:
            @pl.when((y == 0) & (c == 0) & (z == (8 - d) % 8))
            def _():
                zero[p][...] = zs[p][d][0]
        if k == len(ARRIVAL) - 1:
            push_zero(p)

    def n_copy(p, g_there, sem, dev):
        return remote(zero[p], rp[p].at[g_there * SPAN + 8], nsend.at[p, sem], nrecv.at[p], dev)

    def push_zero(p):
        @pl.when((y == 0) & (c == 0))
        def _():
            for dy in range(1, NY):
                for c2 in range(NC):
                    g = 2 * dy - 1 + c2
                    n_copy(p, 2 * dy - 1, g, at(dy, z, c2)).start()
            n_copy(p, 0, 0, other).start()
            rp[p][7 * SPAN + 8] = zero[p][...]

    def y_wait(p):
        whole = (0, 8)
        y_copy(p, 0, 0, whole, other).wait_recv()
        for dy in range(1, NY):
            @pl.when(y >= dy)
            def _():
                for c2 in range(NC):
                    g = 2 * dy - 1 + c2
                    y_copy(p, g, g, whole, other).wait_recv()
                    if c2 == 0:
                        @pl.when(y == dy)
                        def _():
                            n_copy(p, g, g, other).wait_recv()
        @pl.when((y == 0) & (c == 1))
        def _():
            n_copy(p, 0, 0, other).wait_recv()

    cut = (slots + 1) // 2
    spans = (pl.ds(blocks, cut), pl.ds(blocks + cut, slots - cut))

    def compact(p):
        zero_group = jnp.where(y == 0, jnp.where(c == 0, 7, 0), 2 * y - 1)
        tiles[p][blocks, x] = rp[p][zero_group * SPAN + 8]
        for b in range(blocks):
            for j in range(picks):
                tiles[p][blocks + 1 + b * picks + j, x] = rp[p][slot_source(b, j)]

    def x_copy(p, span, of, sem, way):
        region = tiles[p].at[spans[span], of]
        return remote(region, region, xsend.at[p, sem], xrecv.at[p, sem], (x_right, x_left)[way])

    def x_start(p):
        x_copy(p, 0, x, 0, 0).start()
        x_copy(p, 1, x, 3, 1).start()
        x_copy(p, 1, x, 1, 0).start()
        x_copy(p, 0, x, 2, 1).start()

    def x_forward(p):
        x_copy(p, 0, xl, 0, 0).wait_recv()
        x_copy(p, 0, xl, 4, 0).start()
        x_copy(p, 1, xr, 3, 1).wait_recv()
        x_copy(p, 1, xr, 5, 1).start()

    def x_finish(p):
        x_copy(p, 1, xl, 1, 0).wait_recv()
        x_copy(p, 0, xr, 2, 1).wait_recv()
        x_copy(p, 0, xo, 4, 0).wait_recv()
        x_copy(p, 1, xo, 5, 1).wait_recv()

    factor = math.log2(math.e) / math.sqrt(head)
    lanes = 128

    def score(q, keys):
        return lax.dot_general(q, keys, (((1,), (1,)), ((), ())), preferred_element_type=jnp.float32)

    def chunks(b):
        for h in range(heads):
            for r in range(2):
                start = pl.multiple_of(b * block_len, block_len) + r * half
                yield (b * heads + h) * 2 + r, r, pl.ds(start, half), pl.ds(h * head, head)

    def own_part(b0, b1):
        def body(b, _):
            for i, r, at_rows, at_head in chunks(b):
                own = (r + 1) * half
                t = score(q_vm[at_rows, at_head], k_vm[b].reshape(block_len, head)[:own])
                row = lax.broadcasted_iota(jnp.int32, (half, own), 0) + r * half
                col = lax.broadcasted_iota(jnp.int32, (half, own), 1)
                t = jnp.where(col <= row, t, -1e30)
                top = jnp.broadcast_to(jnp.max(t, axis=1, keepdims=True), (half, lanes))
                m_ref[i] = top
                shift = top * factor
                total = jnp.zeros((half, lanes), jnp.float32)
                out = jnp.zeros((half, head), jnp.float32)
                ps = []
                for n in range(own // lanes):
                    e = jnp.exp2(t[:, n * lanes:(n + 1) * lanes] * factor - shift)
                    total += e
                    ps.append(e.astype(jnp.bfloat16))
                l_ref[i] = total
                acc_ref[i] = jnp.dot(
                    jnp.concatenate(ps, axis=1),
                    v_vm[b].reshape(block_len, head)[:own],
                    preferred_element_type=jnp.float32,
                )
            return 0

        lax.fori_loop(b0, b1, body, 0)

    width = NX * rows
    pair = half // width

    def joined(p, picked, g):
        return jnp.concatenate(
            [tiles[p][picked[g * pair + n]].reshape(width, head) for n in range(pair)], axis=0
        )

    groups = (picks + 1) // pair

    def soft_part(p, b0, b1):
        last = p == PARTS - 2

        def body(b, _):
            picked = [tile_of(b, j) for j in range(picks + 1)]
            weight = [jnp.where(tile == null, 0.0, 1.0) for tile in picked]
            for i, r, at_rows, at_head in chunks(b):
                q = q_vm[at_rows, at_head]
                old = m_ref[i]
                top = old
                for g in range(groups):
                    t = score(q, joined(p, picked, g))
                    sc[:, pl.ds(g * half, half)] = t
                    top = jnp.maximum(top, jnp.max(t, axis=1, keepdims=True))
                shift = top * factor
                scale = jnp.exp2(old * factor - shift)
                total = l_ref[i] * scale
                for j in range(picks + 1):
                    for n in range(j * width // lanes, (j + 1) * width // lanes):
                        e = jnp.exp2(sc[:, pl.ds(n * lanes, lanes)] * factor - shift)
                        total += e * weight[j]
                        prob[i, :, pl.ds(n * lanes, lanes)] = e.astype(jnp.bfloat16)
                if last:
                    full = jnp.sum(total, axis=1, keepdims=True)
                    total = jnp.broadcast_to(1.0 / full, (half, lanes))
                l_ref[i] = total
                m_ref[i] = top
                scale_ref[i] = scale
            return 0

        lax.fori_loop(b0, b1, body, 0)

    def out_copy(b):
        at_rows = pl.ds(pl.multiple_of(b * block_len, block_len), block_len)
        return pltpu.make_async_copy(out_vm.at[at_rows], out_hbm.at[at_rows], out_sem.at[b])

    def value_part(p, b0, b1):
        last = p == PARTS - 1

        def body(b, _):
            picked = [tile_of(b, j) for j in range(picks + 1)]
            for h in range(heads):
                i = pl.ds((b * heads + h) * 2, 2)
                out = (acc_ref[i] * scale_ref[i]).reshape(block_len, head)
                for g in range(groups):
                    out += jnp.dot(
                        prob[i, :, pl.ds(g * half, half)].reshape(block_len, half),
                        joined(p, picked, g),
                        preferred_element_type=jnp.float32,
                    )
                if last:
                    out = out * l_ref[i].reshape(block_len, lanes)
                    at_rows = pl.ds(pl.multiple_of(b * block_len, block_len), block_len)
                    out_vm[at_rows, pl.ds(h * head, head)] = out.astype(jnp.bfloat16)
                else:
                    acc_ref[i] = out.reshape(2, half, head)
            if last:
                out_copy(b).start()
            return 0

        lax.fori_loop(b0, b1, body, 0)

    def attend_part(p, b0, b1):
        (soft_part, value_part)[p % 2](p, b0, b1)

    def null_tiles():
        first_key = jnp.broadcast_to(tiles[0][blocks, 0, :1, :].reshape(1, 1, head), (NX, rows, head))
        for p in range(0, PARTS, 2):
            tiles[p][null] = first_key
            tiles[p + 1][null] = jnp.zeros((NX, rows, head), jnp.bfloat16)

    def arrived(p):
        y_wait(p)
        compact(p)
        x_start(p)

    for copy in loads[PARTS:]:
        copy.wait()
    z_wait(0, 1)
    z_start(0, 2)
    push(0, 0)
    z_wait(1, 1)
    z_start(1, 2)
    push(1, 0)
    own_part(0, 1)
    z_wait(0, 2)
    z_start(0, 3)
    push(0, 1)
    z_wait(1, 2)
    z_start(1, 3)
    own_part(1, 2)
    z_wait(0, 3)
    z_start(0, 4)
    z_start(2, 1)
    own_part(2, 3)
    z_wait(0, 4)
    push(0, 2)
    z_wait(1, 3)
    z_start(1, 4)
    push(1, 1)
    z_wait(2, 1)
    z_start(2, 2)
    arrived(0)
    z_wait(1, 4)
    push(1, 2)
    z_start(3, 1)
    own_part(3, 4)
    z_wait(2, 2)
    z_start(2, 3)
    push(2, 0)
    x_forward(0)
    z_wait(3, 1)
    z_start(3, 2)
    push(2, 1)
    arrived(1)
    z_wait(2, 3)
    z_start(2, 4)
    own_part(4, 6)
    z_wait(2, 4)
    push(2, 2)
    z_wait(3, 2)
    z_start(3, 3)
    push(3, 0)
    x_forward(1)
    push(3, 1)
    x_finish(0)
    null_tiles()
    attend_part(0, 0, 1)
    z_wait(3, 3)
    z_start(3, 4)
    attend_part(0, 1, 2)
    arrived(2)
    z_wait(3, 4)
    push(3, 2)
    attend_part(0, 2, 4)
    x_forward(2)
    attend_part(0, 4, 6)
    x_finish(1)
    attend_part(1, 0, 6)
    arrived(3)
    x_finish(2)
    attend_part(2, 0, 2)
    x_forward(3)
    attend_part(2, 2, 6)
    x_finish(3)
    attend_part(3, 0, 6)

    for p in range(PARTS):
        for k in range(1, 5):
            for copy in z_copies(p, k):
                copy.wait_send()
        whole = (0, 8)
        y_copy(p, 0, 0, whole, other).wait_send()
        for dy in range(1, NY):
            @pl.when(y + dy < NY)
            def _():
                for c2 in range(NC):
                    g = 2 * dy - 1 + c2
                    y_copy(p, g, g, whole, other).wait_send()
        @pl.when((y == 0) & (c == 0))
        def _():
            for g in range(7):
                n_copy(p, 0, g, other).wait_send()
        x_copy(p, 0, x, 0, 0).wait_send()
        x_copy(p, 1, x, 3, 1).wait_send()
        x_copy(p, 1, x, 1, 0).wait_send()
        x_copy(p, 0, x, 2, 1).wait_send()
        x_copy(p, 0, xl, 4, 0).wait_send()
        x_copy(p, 1, xr, 5, 1).wait_send()
    table(0, 0, other).wait_send()
    for dy in range(1, NY):
        @pl.when(y >= dy)
        def _():
            for c2 in range(NC):
                table(0, 2 * dy - 1 + c2, other).wait_send()
    for b in range(blocks):
        out_copy(b).wait()


def shards(queries, keys, values, selected):
    blocks, picks = selected.shape
    head = keys.shape[1]
    block_len = keys.shape[0] // blocks
    heads = queries.shape[1] // head
    rows = block_len // (SETS * NX)
    half = block_len // 2
    slots = blocks * picks + 1
    k5 = keys.reshape(blocks, NX, SETS, rows, head)
    v5 = values.reshape(blocks, NX, SETS, rows, head)
    part = lambda *shape: pltpu.VMEM(shape + (rows, head), jnp.bfloat16)
    wide = lambda *shape: pltpu.VMEM(shape, jnp.float32)
    hbm = pl.BlockSpec(memory_space=pl.ANY)
    dma = pltpu.SemaphoreType.DMA
    chunks = blocks * heads * 2
    return pl.pallas_call(
        functools.partial(fused, blocks, picks, block_len, heads),
        out_shape=jax.ShapeDtypeStruct(queries.shape, jnp.bfloat16),
        in_specs=[pl.BlockSpec(memory_space=pltpu.SMEM), hbm, hbm, hbm],
        out_specs=hbm,
        scratch_shapes=[part(blocks)] * (PARTS * NZ)
        + [part(7 * SPAN)] * PARTS
        + [part(GROUPS * SPAN)] * PARTS
        + [part()] * PARTS
        + [part(blocks + slots + 1, NX)] * PARTS
        + [
            pltpu.VMEM(queries.shape, jnp.bfloat16),
            part(blocks, NX, SETS), part(blocks, NX, SETS),
            pltpu.VMEM(queries.shape, jnp.bfloat16),
            pltpu.VMEM((chunks, half, (picks + 1) * NX * rows), jnp.bfloat16),
            wide(half, (picks + 1) * NX * rows),
            wide(chunks, half, 128), wide(chunks, half, 128), wide(chunks, half, head), wide(chunks, half, 128),
            pltpu.VMEM((8, 128), jnp.int32),
            pltpu.VMEM((8, 128), jnp.int32), pltpu.SMEM((8, 128), jnp.int32),
            dma((2 * PARTS + 3,)), dma((1,)),
            dma((PARTS, 4, 2)), dma((PARTS, 4, 2)),
            dma((PARTS, 7)), dma((PARTS, 7)), dma((PARTS, 7)), dma((PARTS,)),
            dma((7,)), dma((7,)), dma((PARTS, 6)), dma((PARTS, 6)), dma((blocks,)),
        ],
        compiler_params=pltpu.CompilerParams(
            collective_id=0, has_side_effects=True, vmem_limit_bytes=56 * 2**20
        ),
    )(selected.T, queries, k5, v5)


def solution(mesh):
    in_specs = (P("seq", "head"), P("seq", None), P("seq", None), P("seq", None))
    return jax.shard_map(shards, mesh=mesh, in_specs=in_specs, out_specs=P("seq", "head"), check_vma=False)
```

```python
import functools
import math

import jax
import jax.numpy as jnp
from jax import lax
from jax.experimental import pallas as pl
from jax.experimental.pallas import tpu as pltpu
from jax.sharding import PartitionSpec as P

MESH = pl.DeviceIdType.MESH
NY, NZ, NC, NX = 4, 8, 2, 4
GROUPS = 8
SPAN = 9
ARRIVAL = ((0, 7, 1), (6, 2), (5, 3, 4))
STARTS = (0, 3, 5)
SETS = 2
TILES = 2 * SETS
PARTS = ((0, 0, 64), (1, 0, 64), (2, 0, 64), (3, 0, 32), (3, 32, 32))


def fused(blocks, picks, block_len, heads, sel, q_hbm, k_hbm, v_hbm, out_hbm, *scratch):
    rows = block_len // (SETS * NX)
    half = block_len // 2
    head = k_hbm.shape[-1]
    slots = blocks * picks + 1
    null = blocks + slots
    scratch = list(scratch)
    take = lambda n: [scratch.pop(0) for _ in range(n)]
    count = len(PARTS)
    zs = [take(NZ) for _ in range(count)]
    sp, rp, zero, tiles = take(count), take(count), take(count), take(TILES)
    (q_vm, k_vm, v_vm, out_vm, prob, sc, m_ref, l_ref, acc_ref, scale_ref, want_ref,
     tabs, tabs_smem, load_sem, tab_local, zsend, zrecv, ysend, yrecv, nsend, nrecv,
     tsend, trecv, xsend, xrecv, out_sem) = scratch
    s = lax.axis_index("seq")
    x = lax.axis_index("head")
    c = lax.rem(s, NC)
    z = lax.rem(s // NC, NZ)
    y = s // (NC * NZ)

    def at(y2, z2, c2):
        return ((y2 * NZ + z2) * NC + c2, x)

    zr, zl = lax.rem(z + 1, NZ), lax.rem(z + NZ - 1, NZ)
    xr, xl, xo = lax.rem(x + 1, NX), lax.rem(x + NX - 1, NX), lax.rem(x + 2, NX)
    right, left = at(y, zr, c), at(y, zl, c)
    other = at(y, z, 1 - c)
    x_right, x_left = (s, xr), (s, xl)

    def remote(src, dst, ss, rs, dev):
        return pltpu.make_async_remote_copy(
            src_ref=src, dst_ref=dst, send_sem=ss, recv_sem=rs, device_id=dev, device_id_type=MESH
        )

    def source(tile):
        return (k_hbm, v_hbm)[tile % 2]

    loads = []
    for p, (tile, row, size) in enumerate(PARTS):
        loads.append(
            pltpu.make_async_copy(
                source(tile).at[:, x, tile // 2, pl.ds(row, size)], zs[p][0], load_sem.at[p]
            )
        )
    for tile in range(TILES):
        loads.append(
            pltpu.make_async_copy(
                source(tile).at[:, :, tile // 2], tiles[tile].at[pl.ds(0, blocks)], load_sem.at[count + tile]
            )
        )
    loads.append(pltpu.make_async_copy(k_hbm, k_vm, load_sem.at[count + TILES]))
    loads.append(pltpu.make_async_copy(v_hbm, v_vm, load_sem.at[count + TILES + 1]))
    loads.append(pltpu.make_async_copy(q_hbm, q_vm, load_sem.at[count + TILES + 2]))
    for copy in loads:
        copy.start()

    lane = lax.broadcasted_iota(jnp.int32, (8, 128), 1)
    want = jnp.zeros((8, 128), jnp.int32)
    for b in range(blocks):
        for j in range(picks):
            chosen = sel[j, b]
            owner = jnp.where(chosen != 0, chosen // blocks, -1)
            want = jnp.where(lane == owner, lax.rem(chosen, blocks), want)
    want_ref[...] = jnp.where(lane == s, 0, want)
    tabs[...] = jnp.where(lane == s, 0, want)

    barrier = pltpu.get_barrier_semaphore()
    partners = [right, left, other, x_right, x_left]
    for dy in range(1, NY):
        for c2 in range(NC):
            partners.append(at(lax.rem(y + dy, NY), z, c2))
    for dev in partners:
        pl.semaphore_signal(barrier, inc=1, device_id=dev, device_id_type=MESH)

    def live(b, j):
        chosen = sel[j, b]
        ok = chosen != 0
        for i in range(j):
            ok = ok & (chosen != sel[i, b])
        return ok

    def slot_source(b, j):
        owner = sel[j, b] // blocks
        oy, oz, oc = owner // (NZ * NC), lax.rem(owner // NC, NZ), lax.rem(owner, NC)
        dy, dz = y - oy, lax.rem(oz - z + NZ, NZ)
        group = jnp.where(dy == 0, jnp.where(oc == c, 7, 0), 2 * dy - 1 + oc)
        place = jnp.where(dz < 4, 2 * dz, jnp.where(dz == 4, 7, 2 * (NZ - dz) - 1))
        return jnp.where(live(b, j) & (owner != s), group * SPAN + place, 7 * SPAN)

    def tile_of(b, j):
        if j == 0:
            return jnp.where(s * blocks + b != 0, blocks, null)
        chosen = sel[j - 1, b]
        here = jnp.where(chosen // blocks == s, lax.rem(chosen, blocks), blocks + 1 + b * picks + (j - 1))
        return jnp.where(live(b, j - 1), here, null)

    for copy in loads[:count]:
        copy.wait()
    pl.semaphore_wait(barrier, len(partners))

    def z_copies(p, k):
        if k < 4:
            a = remote(zs[p][(9 - k) % 8], zs[p][8 - k], zsend.at[p, k - 1, 0], zrecv.at[p, k - 1, 0], right)
            b = remote(zs[p][k - 1], zs[p][k], zsend.at[p, k - 1, 1], zrecv.at[p, k - 1, 1], left)
        else:
            lo, hi = pl.ds(0, blocks // 2), pl.ds(blocks // 2, blocks - blocks // 2)
            a = remote(zs[p][5].at[lo], zs[p][4].at[lo], zsend.at[p, 3, 0], zrecv.at[p, 3, 0], right)
            b = remote(zs[p][3].at[hi], zs[p][4].at[hi], zsend.at[p, 3, 1], zrecv.at[p, 3, 1], left)
        return a, b

    def z_start(p, k):
        for copy in z_copies(p, k):
            copy.start()

    def z_wait(p, k):
        for copy in z_copies(p, k):
            copy.wait_recv()

    z_start(0, 1)

    def table(g_there, sem, dev):
        return remote(want_ref.at[0], tabs.at[g_there], tsend.at[sem], trecv.at[g_there], dev)

    table(0, 0, other).start()
    for dy in range(1, NY):
        @pl.when(y >= dy)
        def _():
            for c2 in range(NC):
                table(2 * dy - 1 + c, 2 * dy - 1 + c2, at(y - dy, z, c2)).start()
    z_start(1, 1)
    table(0, 0, other).wait_recv()
    for dy in range(1, NY):
        @pl.when(y + dy < NY)
        def _():
            for c2 in range(NC):
                g = 2 * dy - 1 + c2
                table(g, g, other).wait_recv()
    tables_in = pltpu.make_async_copy(tabs, tabs_smem, tab_local.at[0])
    tables_in.start()
    tables_in.wait()

    def y_copy(p, g_here, g_there, place, dev):
        return remote(
            sp[p].at[pl.ds(g_here * SPAN + place[0], place[1])],
            rp[p].at[pl.ds(g_there * SPAN + place[0], place[1])],
            ysend.at[p, g_here], yrecv.at[p, g_there], dev,
        )

    def owner_at(d):
        return (y * NZ + lax.rem(z + d, NZ)) * NC + c

    def push(p, k):
        place = (STARTS[k], len(ARRIVAL[k]))

        def pack(g):
            for j, d in enumerate(ARRIVAL[k]):
                sp[p][g * SPAN + place[0] + j] = zs[p][d][tabs_smem[g, owner_at(d)]]

        for dy in (2, 1, 3):
            @pl.when(y + dy < NY)
            def _():
                for c2 in range(NC):
                    g = 2 * dy - 1 + c2
                    pack(g)
                    y_copy(p, g, 2 * dy - 1 + c, place, at(y + dy, z, c2)).start()
        pack(0)
        y_copy(p, 0, 0, place, other).start()
        for j, d in enumerate(ARRIVAL[k]):
            rp[p][7 * SPAN + place[0] + j] = zs[p][d][tabs_smem[7, owner_at(d)]]
        for d in ARRIVAL[k]:
            @pl.when((y == 0) & (c == 0) & (z == (8 - d) % 8))
            def _():
                zero[p][...] = zs[p][d][0]
        if k == len(ARRIVAL) - 1:
            push_zero(p)

    def n_copy(p, g_there, sem, dev):
        return remote(zero[p], rp[p].at[g_there * SPAN + 8], nsend.at[p, sem], nrecv.at[p], dev)

    def push_zero(p):
        @pl.when((y == 0) & (c == 0))
        def _():
            for dy in range(1, NY):
                for c2 in range(NC):
                    g = 2 * dy - 1 + c2
                    n_copy(p, 2 * dy - 1, g, at(dy, z, c2)).start()
            n_copy(p, 0, 0, other).start()
            rp[p][7 * SPAN + 8] = zero[p][...]

    def y_wait(p):
        whole = (0, 8)
        y_copy(p, 0, 0, whole, other).wait_recv()
        for dy in range(1, NY):
            @pl.when(y >= dy)
            def _():
                for c2 in range(NC):
                    g = 2 * dy - 1 + c2
                    y_copy(p, g, g, whole, other).wait_recv()
                    if c2 == 0:
                        @pl.when(y == dy)
                        def _():
                            n_copy(p, g, g, other).wait_recv()
        @pl.when((y == 0) & (c == 1))
        def _():
            n_copy(p, 0, 0, other).wait_recv()

    cut = (slots + 1) // 2
    spans = (pl.ds(blocks, cut), pl.ds(blocks + cut, slots - cut))

    def compact(p):
        zero_group = jnp.where(y == 0, jnp.where(c == 0, 7, 0), 2 * y - 1)
        tile, row, size = PARTS[p]
        tiles[tile][blocks, x, row:row + size] = rp[p][zero_group * SPAN + 8]
        for b in range(blocks):
            for j in range(picks):
                tiles[tile][blocks + 1 + b * picks + j, x, row:row + size] = rp[p][slot_source(b, j)]

    def x_copy(p, span, of, sem, way):
        tile, row, size = PARTS[p]
        region = tiles[tile].at[spans[span], of, pl.ds(row, size)]
        return remote(region, region, xsend.at[p, sem], xrecv.at[p, sem], (x_right, x_left)[way])

    def x_start(p):
        x_copy(p, 0, x, 0, 0).start()
        x_copy(p, 1, x, 3, 1).start()
        x_copy(p, 1, x, 1, 0).start()
        x_copy(p, 0, x, 2, 1).start()

    def x_forward(p):
        x_copy(p, 0, xl, 0, 0).wait_recv()
        x_copy(p, 0, xl, 4, 0).start()
        x_copy(p, 1, xr, 3, 1).wait_recv()
        x_copy(p, 1, xr, 5, 1).start()

    def x_finish(p):
        x_copy(p, 1, xl, 1, 0).wait_recv()
        x_copy(p, 0, xr, 2, 1).wait_recv()
        x_copy(p, 0, xo, 4, 0).wait_recv()
        x_copy(p, 1, xo, 5, 1).wait_recv()

    factor = math.log2(math.e) / math.sqrt(head)
    lanes = 128

    def score(q, keys):
        return lax.dot_general(q, keys, (((1,), (1,)), ((), ())), preferred_element_type=jnp.float32)

    def chunks(b):
        for h in range(heads):
            for r in range(2):
                start = pl.multiple_of(b * block_len, block_len) + r * half
                yield (b * heads + h) * 2 + r, r, pl.ds(start, half), pl.ds(h * head, head)

    def own_part(b0, b1):
        def body(b, _):
            for i, r, at_rows, at_head in chunks(b):
                own = (r + 1) * half
                t = score(q_vm[at_rows, at_head], k_vm[b].reshape(block_len, head)[:own])
                row = lax.broadcasted_iota(jnp.int32, (half, own), 0) + r * half
                col = lax.broadcasted_iota(jnp.int32, (half, own), 1)
                t = jnp.where(col <= row, t, -1e30)
                top = jnp.broadcast_to(jnp.max(t, axis=1, keepdims=True), (half, lanes))
                m_ref[i] = top
                shift = top * factor
                total = jnp.zeros((half, lanes), jnp.float32)
                out = jnp.zeros((half, head), jnp.float32)
                ps = []
                for n in range(own // lanes):
                    e = jnp.exp2(t[:, n * lanes:(n + 1) * lanes] * factor - shift)
                    total += e
                    ps.append(e.astype(jnp.bfloat16))
                l_ref[i] = total
                acc_ref[i] = jnp.dot(
                    jnp.concatenate(ps, axis=1),
                    v_vm[b].reshape(block_len, head)[:own],
                    preferred_element_type=jnp.float32,
                )
            return 0

        lax.fori_loop(b0, b1, body, 0)

    width = NX * rows
    pair = half // width

    def joined(p, picked, g):
        return jnp.concatenate(
            [tiles[p][picked[g * pair + n]].reshape(width, head) for n in range(pair)], axis=0
        )

    groups = (picks + 1) // pair

    def soft_part(p, b0, b1):
        last = p == TILES - 2

        def body(b, _):
            picked = [tile_of(b, j) for j in range(picks + 1)]
            weight = [jnp.where(tile == null, 0.0, 1.0) for tile in picked]
            for i, r, at_rows, at_head in chunks(b):
                q = q_vm[at_rows, at_head]
                old = m_ref[i]
                top = old
                for g in range(groups):
                    t = score(q, joined(p, picked, g))
                    sc[:, pl.ds(g * half, half)] = t
                    top = jnp.maximum(top, jnp.max(t, axis=1, keepdims=True))
                shift = top * factor
                scale = jnp.exp2(old * factor - shift)
                total = l_ref[i] * scale
                for j in range(picks + 1):
                    for n in range(j * width // lanes, (j + 1) * width // lanes):
                        e = jnp.exp2(sc[:, pl.ds(n * lanes, lanes)] * factor - shift)
                        total += e * weight[j]
                        prob[i, :, pl.ds(n * lanes, lanes)] = e.astype(jnp.bfloat16)
                if last:
                    full = jnp.sum(total, axis=1, keepdims=True)
                    total = jnp.broadcast_to(1.0 / full, (half, lanes))
                l_ref[i] = total
                m_ref[i] = top
                scale_ref[i] = scale
            return 0

        lax.fori_loop(b0, b1, body, 0)

    def out_copy(b):
        at_rows = pl.ds(pl.multiple_of(b * block_len, block_len), block_len)
        return pltpu.make_async_copy(out_vm.at[at_rows], out_hbm.at[at_rows], out_sem.at[b])

    def value_part(p, b0, b1):
        last = p == TILES - 1

        def body(b, _):
            picked = [tile_of(b, j) for j in range(picks + 1)]
            for h in range(heads):
                i = pl.ds((b * heads + h) * 2, 2)
                out = (acc_ref[i] * scale_ref[i]).reshape(block_len, head)
                for g in range(groups):
                    out += jnp.dot(
                        prob[i, :, pl.ds(g * half, half)].reshape(block_len, half),
                        joined(p, picked, g),
                        preferred_element_type=jnp.float32,
                    )
                if last:
                    out = out * l_ref[i].reshape(block_len, lanes)
                    at_rows = pl.ds(pl.multiple_of(b * block_len, block_len), block_len)
                    out_vm[at_rows, pl.ds(h * head, head)] = out.astype(jnp.bfloat16)
                else:
                    acc_ref[i] = out.reshape(2, half, head)
            if last:
                out_copy(b).start()
            return 0

        lax.fori_loop(b0, b1, body, 0)

    def attend_part(p, b0, b1):
        (soft_part, value_part)[p % 2](p, b0, b1)

    def null_tiles():
        first_key = jnp.broadcast_to(tiles[0][blocks, 0, :1, :].reshape(1, 1, head), (NX, rows, head))
        for p in range(0, TILES, 2):
            tiles[p][null] = first_key
            tiles[p + 1][null] = jnp.zeros((NX, rows, head), jnp.bfloat16)

    def arrived(p):
        y_wait(p)
        compact(p)
        x_start(p)

    for copy in loads[count:]:
        copy.wait()
    z_wait(0, 1)
    z_start(0, 2)
    push(0, 0)
    z_wait(1, 1)
    z_start(1, 2)
    push(1, 0)
    own_part(0, 1)
    z_wait(0, 2)
    z_start(0, 3)
    push(0, 1)
    z_wait(1, 2)
    z_start(1, 3)
    own_part(1, 2)
    z_wait(0, 3)
    z_start(0, 4)
    z_start(2, 1)
    own_part(2, 3)
    z_wait(0, 4)
    push(0, 2)
    z_wait(1, 3)
    z_start(1, 4)
    push(1, 1)
    z_wait(2, 1)
    z_start(2, 2)
    arrived(0)
    z_wait(1, 4)
    push(1, 2)
    z_start(3, 1)
    z_start(4, 1)
    own_part(3, 4)
    z_wait(2, 2)
    z_start(2, 3)
    push(2, 0)
    x_forward(0)
    z_wait(3, 1)
    z_start(3, 2)
    push(2, 1)
    z_wait(4, 1)
    z_start(4, 2)
    arrived(1)
    z_wait(2, 3)
    z_start(2, 4)
    own_part(4, 6)
    z_wait(2, 4)
    push(2, 2)
    z_wait(3, 2)
    z_start(3, 3)
    push(3, 0)
    z_wait(4, 2)
    z_start(4, 3)
    push(3, 1)
    x_finish(0)
    null_tiles()
    attend_part(0, 0, 1)
    x_forward(1)
    attend_part(0, 1, 2)
    z_wait(3, 3)
    z_start(3, 4)
    z_wait(4, 3)
    z_start(4, 4)
    push(4, 0)
    attend_part(0, 2, 3)
    arrived(2)
    z_wait(3, 4)
    push(3, 2)
    z_wait(4, 4)
    push(4, 1)
    push(4, 2)
    attend_part(0, 3, 5)
    x_forward(2)
    attend_part(0, 5, 6)
    x_finish(1)
    attend_part(1, 0, 2)
    arrived(3)
    attend_part(1, 2, 6)
    x_finish(2)
    attend_part(2, 0, 1)
    arrived(4)
    x_forward(3)
    attend_part(2, 1, 3)
    x_forward(4)
    attend_part(2, 3, 6)
    x_finish(3)
    x_finish(4)
    attend_part(3, 0, 6)

    for p in range(count):
        for k in range(1, 5):
            for copy in z_copies(p, k):
                copy.wait_send()
        whole = (0, 8)
        y_copy(p, 0, 0, whole, other).wait_send()
        for dy in range(1, NY):
            @pl.when(y + dy < NY)
            def _():
                for c2 in range(NC):
                    g = 2 * dy - 1 + c2
                    y_copy(p, g, g, whole, other).wait_send()
        @pl.when((y == 0) & (c == 0))
        def _():
            for g in range(7):
                n_copy(p, 0, g, other).wait_send()
        x_copy(p, 0, x, 0, 0).wait_send()
        x_copy(p, 1, x, 3, 1).wait_send()
        x_copy(p, 1, x, 1, 0).wait_send()
        x_copy(p, 0, x, 2, 1).wait_send()
        x_copy(p, 0, xl, 4, 0).wait_send()
        x_copy(p, 1, xr, 5, 1).wait_send()
    table(0, 0, other).wait_send()
    for dy in range(1, NY):
        @pl.when(y >= dy)
        def _():
            for c2 in range(NC):
                table(0, 2 * dy - 1 + c2, other).wait_send()
    for b in range(blocks):
        out_copy(b).wait()


def shards(queries, keys, values, selected):
    blocks, picks = selected.shape
    head = keys.shape[1]
    block_len = keys.shape[0] // blocks
    heads = queries.shape[1] // head
    rows = block_len // (SETS * NX)
    half = block_len // 2
    slots = blocks * picks + 1
    k5 = keys.reshape(blocks, NX, SETS, rows, head)
    v5 = values.reshape(blocks, NX, SETS, rows, head)
    part = lambda *shape: pltpu.VMEM(shape + (rows, head), jnp.bfloat16)
    sized = lambda *shape: [pltpu.VMEM(shape + (size, head), jnp.bfloat16) for _, _, size in PARTS]
    count = len(PARTS)
    wide = lambda *shape: pltpu.VMEM(shape, jnp.float32)
    hbm = pl.BlockSpec(memory_space=pl.ANY)
    dma = pltpu.SemaphoreType.DMA
    chunks = blocks * heads * 2
    return pl.pallas_call(
        functools.partial(fused, blocks, picks, block_len, heads),
        out_shape=jax.ShapeDtypeStruct(queries.shape, jnp.bfloat16),
        in_specs=[pl.BlockSpec(memory_space=pltpu.SMEM), hbm, hbm, hbm],
        out_specs=hbm,
        scratch_shapes=[ref for ref in sized(blocks) for _ in range(NZ)]
        + sized(7 * SPAN)
        + sized(GROUPS * SPAN)
        + sized()
        + [part(blocks + slots + 1, NX)] * TILES
        + [
            pltpu.VMEM(queries.shape, jnp.bfloat16),
            part(blocks, NX, SETS), part(blocks, NX, SETS),
            pltpu.VMEM(queries.shape, jnp.bfloat16),
            pltpu.VMEM((chunks, half, (picks + 1) * NX * rows), jnp.bfloat16),
            wide(half, (picks + 1) * NX * rows),
            wide(chunks, half, 128), wide(chunks, half, 128), wide(chunks, half, head), wide(chunks, half, 128),
            pltpu.VMEM((8, 128), jnp.int32),
            pltpu.VMEM((8, 128), jnp.int32), pltpu.SMEM((8, 128), jnp.int32),
            dma((count + TILES + 3,)), dma((1,)),
            dma((count, 4, 2)), dma((count, 4, 2)),
            dma((count, 7)), dma((count, 7)), dma((count, 7)), dma((count,)),
            dma((7,)), dma((7,)), dma((count, 6)), dma((count, 6)), dma((blocks,)),
        ],
        compiler_params=pltpu.CompilerParams(
            collective_id=0, has_side_effects=True, vmem_limit_bytes=56 * 2**20
        ),
    )(selected.T, queries, k5, v5)


def solution(mesh):
    in_specs = (P("seq", "head"), P("seq", None), P("seq", None), P("seq", None))
    return jax.shard_map(shards, mesh=mesh, in_specs=in_specs, out_specs=P("seq", "head"), check_vma=False)
```

```python
import functools
import math

import jax
import jax.numpy as jnp
from jax import lax
from jax.experimental import pallas as pl
from jax.experimental.pallas import tpu as pltpu
from jax.sharding import PartitionSpec as P

MESH = pl.DeviceIdType.MESH
NY, NZ, NC, NX = 4, 8, 2, 4
GROUPS = 8
SPAN = 9
ARRIVAL = ((0, 7, 1), (6, 2), (5, 3, 4))
STARTS = (0, 3, 5)
SETS = 2
TILES = 2 * SETS
PARTS = ((0, 0, 64), (1, 0, 64), (2, 0, 64), (3, 0, 32), (3, 32, 32))


def fused(blocks, picks, block_len, heads, sel, q_hbm, k_hbm, v_hbm, out_hbm, *scratch):
    rows = block_len // (SETS * NX)
    half = block_len // 2
    head = k_hbm.shape[-1]
    slots = blocks * picks + 1
    null = blocks + slots
    scratch = list(scratch)
    take = lambda n: [scratch.pop(0) for _ in range(n)]
    count = len(PARTS)
    zs = [take(NZ) for _ in range(count)]
    sp, rp, zero, tiles = take(count), take(count), take(count), take(TILES)
    (q_vm, k_vm, v_vm, out_vm, prob, sc, m_ref, l_ref, acc_ref, scale_ref, want_ref,
     tabs, tabs_smem, load_sem, tab_local, zsend, zrecv, ysend, yrecv, nsend, nrecv,
     tsend, trecv, xsend, xrecv, out_sem) = scratch
    s = lax.axis_index("seq")
    x = lax.axis_index("head")
    c = lax.rem(s, NC)
    z = lax.rem(s // NC, NZ)
    y = s // (NC * NZ)

    def at(y2, z2, c2):
        return ((y2 * NZ + z2) * NC + c2, x)

    zr, zl = lax.rem(z + 1, NZ), lax.rem(z + NZ - 1, NZ)
    xr, xl, xo = lax.rem(x + 1, NX), lax.rem(x + NX - 1, NX), lax.rem(x + 2, NX)
    right, left = at(y, zr, c), at(y, zl, c)
    other = at(y, z, 1 - c)
    x_right, x_left = (s, xr), (s, xl)

    def remote(src, dst, ss, rs, dev):
        return pltpu.make_async_remote_copy(
            src_ref=src, dst_ref=dst, send_sem=ss, recv_sem=rs, device_id=dev, device_id_type=MESH
        )

    def source(tile):
        return (k_hbm, v_hbm)[tile % 2]

    loads = []
    for p, (tile, row, size) in enumerate(PARTS):
        loads.append(
            pltpu.make_async_copy(
                source(tile).at[:, x, tile // 2, pl.ds(row, size)], zs[p][0], load_sem.at[p]
            )
        )
    for tile in range(TILES):
        loads.append(
            pltpu.make_async_copy(
                source(tile).at[:, :, tile // 2], tiles[tile].at[pl.ds(0, blocks)], load_sem.at[count + tile]
            )
        )
    loads.append(pltpu.make_async_copy(k_hbm, k_vm, load_sem.at[count + TILES]))
    loads.append(pltpu.make_async_copy(v_hbm, v_vm, load_sem.at[count + TILES + 1]))
    loads.append(pltpu.make_async_copy(q_hbm, q_vm, load_sem.at[count + TILES + 2]))
    for copy in loads:
        copy.start()

    lane = lax.broadcasted_iota(jnp.int32, (8, 128), 1)
    want = jnp.zeros((8, 128), jnp.int32)
    for b in range(blocks):
        for j in range(picks):
            chosen = sel[j, b]
            owner = jnp.where(chosen != 0, chosen // blocks, -1)
            want = jnp.where(lane == owner, lax.rem(chosen, blocks), want)
    want_ref[...] = jnp.where(lane == s, 0, want)
    tabs[...] = jnp.where(lane == s, 0, want)

    barrier = pltpu.get_barrier_semaphore()
    partners = [right, left, other, x_right, x_left]
    for dy in range(1, NY):
        for c2 in range(NC):
            partners.append(at(lax.rem(y + dy, NY), z, c2))
    for dev in partners:
        pl.semaphore_signal(barrier, inc=1, device_id=dev, device_id_type=MESH)

    def live(b, j):
        chosen = sel[j, b]
        ok = chosen != 0
        for i in range(j):
            ok = ok & (chosen != sel[i, b])
        return ok

    def slot_source(b, j):
        owner = sel[j, b] // blocks
        oy, oz, oc = owner // (NZ * NC), lax.rem(owner // NC, NZ), lax.rem(owner, NC)
        dy, dz = y - oy, lax.rem(oz - z + NZ, NZ)
        group = jnp.where(dy == 0, jnp.where(oc == c, 7, 0), 2 * dy - 1 + oc)
        place = jnp.where(dz < 4, 2 * dz, jnp.where(dz == 4, 7, 2 * (NZ - dz) - 1))
        return jnp.where(live(b, j) & (owner != s), group * SPAN + place, 7 * SPAN)

    def tile_of(b, j):
        if j == 0:
            return jnp.where(s * blocks + b != 0, blocks, null)
        chosen = sel[j - 1, b]
        here = jnp.where(chosen // blocks == s, lax.rem(chosen, blocks), blocks + 1 + b * picks + (j - 1))
        return jnp.where(live(b, j - 1), here, null)

    for copy in loads[:count]:
        copy.wait()
    pl.semaphore_wait(barrier, len(partners))

    def z_copies(p, k):
        if k < 4:
            a = remote(zs[p][(9 - k) % 8], zs[p][8 - k], zsend.at[p, k - 1, 0], zrecv.at[p, k - 1, 0], right)
            b = remote(zs[p][k - 1], zs[p][k], zsend.at[p, k - 1, 1], zrecv.at[p, k - 1, 1], left)
        else:
            lo, hi = pl.ds(0, blocks // 2), pl.ds(blocks // 2, blocks - blocks // 2)
            a = remote(zs[p][5].at[lo], zs[p][4].at[lo], zsend.at[p, 3, 0], zrecv.at[p, 3, 0], right)
            b = remote(zs[p][3].at[hi], zs[p][4].at[hi], zsend.at[p, 3, 1], zrecv.at[p, 3, 1], left)
        return a, b

    def z_start(p, k):
        for copy in z_copies(p, k):
            copy.start()

    def z_wait(p, k):
        for copy in z_copies(p, k):
            copy.wait_recv()

    z_start(0, 1)

    def table(g_there, sem, dev):
        return remote(want_ref.at[0], tabs.at[g_there], tsend.at[sem], trecv.at[g_there], dev)

    table(0, 0, other).start()
    for dy in range(1, NY):
        @pl.when(y >= dy)
        def _():
            for c2 in range(NC):
                table(2 * dy - 1 + c, 2 * dy - 1 + c2, at(y - dy, z, c2)).start()
    z_start(1, 1)
    table(0, 0, other).wait_recv()
    for dy in range(1, NY):
        @pl.when(y + dy < NY)
        def _():
            for c2 in range(NC):
                g = 2 * dy - 1 + c2
                table(g, g, other).wait_recv()
    tables_in = pltpu.make_async_copy(tabs, tabs_smem, tab_local.at[0])
    tables_in.start()
    tables_in.wait()

    def y_copy(p, g_here, g_there, place, dev):
        return remote(
            sp[p].at[pl.ds(g_here * SPAN + place[0], place[1])],
            rp[p].at[pl.ds(g_there * SPAN + place[0], place[1])],
            ysend.at[p, g_here], yrecv.at[p, g_there], dev,
        )

    def owner_at(d):
        return (y * NZ + lax.rem(z + d, NZ)) * NC + c

    def push(p, k):
        place = (STARTS[k], len(ARRIVAL[k]))

        def pack(g):
            for j, d in enumerate(ARRIVAL[k]):
                sp[p][g * SPAN + place[0] + j] = zs[p][d][tabs_smem[g, owner_at(d)]]

        for dy in (2, 1, 3):
            @pl.when(y + dy < NY)
            def _():
                for c2 in range(NC):
                    g = 2 * dy - 1 + c2
                    pack(g)
                    y_copy(p, g, 2 * dy - 1 + c, place, at(y + dy, z, c2)).start()
        pack(0)
        y_copy(p, 0, 0, place, other).start()
        for j, d in enumerate(ARRIVAL[k]):
            rp[p][7 * SPAN + place[0] + j] = zs[p][d][tabs_smem[7, owner_at(d)]]
        for d in ARRIVAL[k]:
            @pl.when((y == 0) & (c == 0) & (z == (8 - d) % 8))
            def _():
                zero[p][...] = zs[p][d][0]
        if k == len(ARRIVAL) - 1:
            push_zero(p)

    def n_copy(p, g_there, sem, dev):
        return remote(zero[p], rp[p].at[g_there * SPAN + 8], nsend.at[p, sem], nrecv.at[p], dev)

    def push_zero(p):
        @pl.when((y == 0) & (c == 0))
        def _():
            for dy in range(1, NY):
                for c2 in range(NC):
                    g = 2 * dy - 1 + c2
                    n_copy(p, 2 * dy - 1, g, at(dy, z, c2)).start()
            n_copy(p, 0, 0, other).start()
            rp[p][7 * SPAN + 8] = zero[p][...]

    def y_wait(p):
        whole = (0, 8)
        y_copy(p, 0, 0, whole, other).wait_recv()
        for dy in range(1, NY):
            @pl.when(y >= dy)
            def _():
                for c2 in range(NC):
                    g = 2 * dy - 1 + c2
                    y_copy(p, g, g, whole, other).wait_recv()
                    if c2 == 0:
                        @pl.when(y == dy)
                        def _():
                            n_copy(p, g, g, other).wait_recv()
        @pl.when((y == 0) & (c == 1))
        def _():
            n_copy(p, 0, 0, other).wait_recv()

    cut = (slots + 1) // 2
    spans = (pl.ds(blocks, cut), pl.ds(blocks + cut, slots - cut))

    def compact(p):
        zero_group = jnp.where(y == 0, jnp.where(c == 0, 7, 0), 2 * y - 1)
        tile, row, size = PARTS[p]
        tiles[tile][blocks, x, row:row + size] = rp[p][zero_group * SPAN + 8]
        for b in range(blocks):
            for j in range(picks):
                tiles[tile][blocks + 1 + b * picks + j, x, row:row + size] = rp[p][slot_source(b, j)]

    def x_copy(p, span, of, sem, way):
        tile, row, size = PARTS[p]
        region = tiles[tile].at[spans[span], of, pl.ds(row, size)]
        return remote(region, region, xsend.at[p, sem], xrecv.at[p, sem], (x_right, x_left)[way])

    def x_start(p):
        x_copy(p, 0, x, 0, 0).start()
        x_copy(p, 1, x, 3, 1).start()
        x_copy(p, 1, x, 1, 0).start()
        x_copy(p, 0, x, 2, 1).start()

    def x_forward(p):
        x_copy(p, 0, xl, 0, 0).wait_recv()
        x_copy(p, 0, xl, 4, 0).start()
        x_copy(p, 1, xr, 3, 1).wait_recv()
        x_copy(p, 1, xr, 5, 1).start()

    def x_finish(p):
        x_copy(p, 1, xl, 1, 0).wait_recv()
        x_copy(p, 0, xr, 2, 1).wait_recv()
        x_copy(p, 0, xo, 4, 0).wait_recv()
        x_copy(p, 1, xo, 5, 1).wait_recv()

    factor = math.log2(math.e) / math.sqrt(head)
    lanes = 128

    def score(q, keys):
        return lax.dot_general(q, keys, (((1,), (1,)), ((), ())), preferred_element_type=jnp.float32)

    def chunks(b):
        for h in range(heads):
            for r in range(2):
                start = pl.multiple_of(b * block_len, block_len) + r * half
                yield (b * heads + h) * 2 + r, r, pl.ds(start, half), pl.ds(h * head, head)

    def own_part(b0, b1):
        def body(b, _):
            for i, r, at_rows, at_head in chunks(b):
                own = (r + 1) * half
                t = score(q_vm[at_rows, at_head], k_vm[b].reshape(block_len, head)[:own])
                row = lax.broadcasted_iota(jnp.int32, (half, own), 0) + r * half
                col = lax.broadcasted_iota(jnp.int32, (half, own), 1)
                t = jnp.where(col <= row, t, -1e30)
                top = jnp.broadcast_to(jnp.max(t, axis=1, keepdims=True), (half, lanes))
                m_ref[i] = top
                shift = top * factor
                total = jnp.zeros((half, lanes), jnp.float32)
                out = jnp.zeros((half, head), jnp.float32)
                ps = []
                for n in range(own // lanes):
                    e = jnp.exp2(t[:, n * lanes:(n + 1) * lanes] * factor - shift)
                    total += e
                    ps.append(e.astype(jnp.bfloat16))
                l_ref[i] = total
                acc_ref[i] = jnp.dot(
                    jnp.concatenate(ps, axis=1),
                    v_vm[b].reshape(block_len, head)[:own],
                    preferred_element_type=jnp.float32,
                )
            return 0

        lax.fori_loop(b0, b1, body, 0)

    width = NX * rows
    pair = half // width

    def joined(p, picked, g):
        return jnp.concatenate(
            [tiles[p][picked[g * pair + n]].reshape(width, head) for n in range(pair)], axis=0
        )

    groups = (picks + 1) // pair

    def soft_part(p, b0, b1):
        last = p == TILES - 2

        def body(b, _):
            picked = [tile_of(b, j) for j in range(picks + 1)]
            weight = [jnp.where(tile == null, 0.0, 1.0) for tile in picked]
            for i, r, at_rows, at_head in chunks(b):
                q = q_vm[at_rows, at_head]
                old = m_ref[i]
                top = old
                for g in range(groups):
                    t = score(q, joined(p, picked, g))
                    sc[:, pl.ds(g * half, half)] = t
                    for n in range(half // lanes):
                        top = jnp.maximum(top, t[:, n * lanes:(n + 1) * lanes])
                top = jnp.broadcast_to(jnp.max(top, axis=1, keepdims=True), (half, lanes))
                shift = top * factor
                scale = jnp.exp2(old * factor - shift)
                total = l_ref[i] * scale
                for j in range(picks + 1):
                    part = jnp.zeros((half, lanes), jnp.float32)
                    for n in range(j * width // lanes, (j + 1) * width // lanes):
                        e = jnp.exp2(sc[:, pl.ds(n * lanes, lanes)] * factor - shift)
                        part += e
                        prob[i, :, pl.ds(n * lanes, lanes)] = e.astype(jnp.bfloat16)
                    total += part * weight[j]
                if last:
                    full = jnp.sum(total, axis=1, keepdims=True)
                    total = jnp.broadcast_to(1.0 / full, (half, lanes))
                l_ref[i] = total
                m_ref[i] = top
                scale_ref[i] = scale
            return 0

        lax.fori_loop(b0, b1, body, 0)

    def out_copy(b):
        at_rows = pl.ds(pl.multiple_of(b * block_len, block_len), block_len)
        return pltpu.make_async_copy(out_vm.at[at_rows], out_hbm.at[at_rows], out_sem.at[b])

    def value_part(p, b0, b1):
        last = p == TILES - 1

        def body(b, _):
            picked = [tile_of(b, j) for j in range(picks + 1)]
            for h in range(heads):
                i = pl.ds((b * heads + h) * 2, 2)
                out = (acc_ref[i] * scale_ref[i]).reshape(block_len, head)
                for g in range(groups):
                    out += jnp.dot(
                        prob[i, :, pl.ds(g * half, half)].reshape(block_len, half),
                        joined(p, picked, g),
                        preferred_element_type=jnp.float32,
                    )
                if last:
                    out = out * l_ref[i].reshape(block_len, lanes)
                    at_rows = pl.ds(pl.multiple_of(b * block_len, block_len), block_len)
                    out_vm[at_rows, pl.ds(h * head, head)] = out.astype(jnp.bfloat16)
                else:
                    acc_ref[i] = out.reshape(2, half, head)
            if last:
                out_copy(b).start()
            return 0

        lax.fori_loop(b0, b1, body, 0)

    def attend_part(p, b0, b1):
        (soft_part, value_part)[p % 2](p, b0, b1)

    def null_tiles():
        first_key = jnp.broadcast_to(tiles[0][blocks, 0, :1, :].reshape(1, 1, head), (NX, rows, head))
        for p in range(0, TILES, 2):
            tiles[p][null] = first_key
            tiles[p + 1][null] = jnp.zeros((NX, rows, head), jnp.bfloat16)

    def arrived(p):
        y_wait(p)
        compact(p)
        x_start(p)

    for copy in loads[count:]:
        copy.wait()
    z_wait(0, 1)
    z_start(0, 2)
    push(0, 0)
    z_wait(1, 1)
    z_start(1, 2)
    push(1, 0)
    own_part(0, 1)
    z_wait(0, 2)
    z_start(0, 3)
    push(0, 1)
    z_wait(1, 2)
    z_start(1, 3)
    own_part(1, 2)
    z_wait(0, 3)
    z_start(0, 4)
    z_start(2, 1)
    own_part(2, 3)
    z_wait(0, 4)
    push(0, 2)
    z_wait(1, 3)
    z_start(1, 4)
    push(1, 1)
    z_wait(2, 1)
    z_start(2, 2)
    arrived(0)
    z_wait(1, 4)
    push(1, 2)
    z_start(3, 1)
    z_start(4, 1)
    own_part(3, 4)
    z_wait(2, 2)
    z_start(2, 3)
    push(2, 0)
    x_forward(0)
    z_wait(3, 1)
    z_start(3, 2)
    push(2, 1)
    z_wait(4, 1)
    z_start(4, 2)
    arrived(1)
    z_wait(2, 3)
    z_start(2, 4)
    own_part(4, 6)
    z_wait(2, 4)
    push(2, 2)
    z_wait(3, 2)
    z_start(3, 3)
    push(3, 0)
    z_wait(4, 2)
    z_start(4, 3)
    push(3, 1)
    x_finish(0)
    null_tiles()
    attend_part(0, 0, 1)
    x_forward(1)
    attend_part(0, 1, 2)
    z_wait(3, 3)
    z_start(3, 4)
    z_wait(4, 3)
    z_start(4, 4)
    push(4, 0)
    attend_part(0, 2, 3)
    arrived(2)
    z_wait(3, 4)
    push(3, 2)
    z_wait(4, 4)
    push(4, 1)
    push(4, 2)
    attend_part(0, 3, 5)
    x_forward(2)
    attend_part(0, 5, 6)
    x_finish(1)
    attend_part(1, 0, 2)
    arrived(3)
    attend_part(1, 2, 6)
    x_finish(2)
    attend_part(2, 0, 1)
    arrived(4)
    x_forward(3)
    attend_part(2, 1, 3)
    x_forward(4)
    attend_part(2, 3, 6)
    x_finish(3)
    x_finish(4)
    attend_part(3, 0, 6)

    for p in range(count):
        for k in range(1, 5):
            for copy in z_copies(p, k):
                copy.wait_send()
        whole = (0, 8)
        y_copy(p, 0, 0, whole, other).wait_send()
        for dy in range(1, NY):
            @pl.when(y + dy < NY)
            def _():
                for c2 in range(NC):
                    g = 2 * dy - 1 + c2
                    y_copy(p, g, g, whole, other).wait_send()
        @pl.when((y == 0) & (c == 0))
        def _():
            for g in range(7):
                n_copy(p, 0, g, other).wait_send()
        x_copy(p, 0, x, 0, 0).wait_send()
        x_copy(p, 1, x, 3, 1).wait_send()
        x_copy(p, 1, x, 1, 0).wait_send()
        x_copy(p, 0, x, 2, 1).wait_send()
        x_copy(p, 0, xl, 4, 0).wait_send()
        x_copy(p, 1, xr, 5, 1).wait_send()
    table(0, 0, other).wait_send()
    for dy in range(1, NY):
        @pl.when(y >= dy)
        def _():
            for c2 in range(NC):
                table(0, 2 * dy - 1 + c2, other).wait_send()
    for b in range(blocks):
        out_copy(b).wait()


def shards(queries, keys, values, selected):
    blocks, picks = selected.shape
    head = keys.shape[1]
    block_len = keys.shape[0] // blocks
    heads = queries.shape[1] // head
    rows = block_len // (SETS * NX)
    half = block_len // 2
    slots = blocks * picks + 1
    k5 = keys.reshape(blocks, NX, SETS, rows, head)
    v5 = values.reshape(blocks, NX, SETS, rows, head)
    part = lambda *shape: pltpu.VMEM(shape + (rows, head), jnp.bfloat16)
    sized = lambda *shape: [pltpu.VMEM(shape + (size, head), jnp.bfloat16) for _, _, size in PARTS]
    count = len(PARTS)
    wide = lambda *shape: pltpu.VMEM(shape, jnp.float32)
    hbm = pl.BlockSpec(memory_space=pl.ANY)
    dma = pltpu.SemaphoreType.DMA
    chunks = blocks * heads * 2
    return pl.pallas_call(
        functools.partial(fused, blocks, picks, block_len, heads),
        out_shape=jax.ShapeDtypeStruct(queries.shape, jnp.bfloat16),
        in_specs=[pl.BlockSpec(memory_space=pltpu.SMEM), hbm, hbm, hbm],
        out_specs=hbm,
        scratch_shapes=[ref for ref in sized(blocks) for _ in range(NZ)]
        + sized(7 * SPAN)
        + sized(GROUPS * SPAN)
        + sized()
        + [part(blocks + slots + 1, NX)] * TILES
        + [
            pltpu.VMEM(queries.shape, jnp.bfloat16),
            part(blocks, NX, SETS), part(blocks, NX, SETS),
            pltpu.VMEM(queries.shape, jnp.bfloat16),
            pltpu.VMEM((chunks, half, (picks + 1) * NX * rows), jnp.bfloat16),
            wide(half, (picks + 1) * NX * rows),
            wide(chunks, half, 128), wide(chunks, half, 128), wide(chunks, half, head), wide(chunks, half, 128),
            pltpu.VMEM((8, 128), jnp.int32),
            pltpu.VMEM((8, 128), jnp.int32), pltpu.SMEM((8, 128), jnp.int32),
            dma((count + TILES + 3,)), dma((1,)),
            dma((count, 4, 2)), dma((count, 4, 2)),
            dma((count, 7)), dma((count, 7)), dma((count, 7)), dma((count,)),
            dma((7,)), dma((7,)), dma((count, 6)), dma((count, 6)), dma((blocks,)),
        ],
        compiler_params=pltpu.CompilerParams(
            collective_id=0, has_side_effects=True, vmem_limit_bytes=56 * 2**20
        ),
    )(selected.T, queries, k5, v5)


def solution(mesh):
    in_specs = (P("seq", "head"), P("seq", None), P("seq", None), P("seq", None))
    return jax.shard_map(shards, mesh=mesh, in_specs=in_specs, out_specs=P("seq", "head"), check_vma=False)
```
